512 devices in a mesh: ctx: 32 (over z, y_hi), dp: 16 (over x, y_lo, core).
Axes of the slice: x: 4, y: 8 (y_hi: 4, y_lo: 2; y = y_hi * 2 + y_lo), z: 8, core: 2. Of those that a mesh axis runs over, the one named last changes fastest.
Arguments:
- queries: bfloat16 [65536, 3584], P(('ctx', 'dp')), may hold values from -17 to 17
- keys: bfloat16 [65536, 512], P(('ctx', 'dp')), may hold values from -17 to 17
- values: bfloat16 [65536, 512], P(('ctx', 'dp')), may hold values from -6 to 6
- d_out: bfloat16 [65536, 3584], P(('ctx', 'dp')), may hold values from -6 to 6
- lengths: int32 [512], replicated, may hold values from 1 to 256, 65536 in all
Outputs:
- attended: bfloat16 [65536, 3584], P(('ctx', 'dp'))
- d_queries: bfloat16 [65536, 3584], P(('ctx', 'dp'))
- d_keys: bfloat16 [65536, 512], P(('ctx', 'dp'))
- d_values: bfloat16 [65536, 512], P(('ctx', 'dp'))
The draws below stay inside these ranges and needn't reach their ends.
Inputs may be any that keep to these rules, and one draw needn't show every extreme that they name: The lengths sum to 65536; the longest is exactly 256.
All inputs are finite; a program needn't handle non-finite values.
Results may differ from the reference program's by a relative error of at most 0.022.
Values may be sent and summed in bfloat16 or wider, within the bound.
No kernel may reach another device: no remote copies, remote signals or barrier semaphores. Data moves between devices by JAX's collectives and lax.ppermute only.
A program may use at most 128 MiB of HBM per device.

```python
import math
import jax
import jax.numpy as jnp
import numpy as np
from jax import lax

QH = 28
KVH = 4
HD = 128
TOK_DEV = 128
DOC_MAX = 256
TOKENS = 65536
DOCS = 512


def shared_rows(key):
    base = jnp.clip(jax.random.normal(key, (TOKENS, KVH * HD), jnp.float32), -4.0, 4.0)
    return base


def draw_keys(key, part):
    base = shared_rows(key)
    return base.astype(jnp.bfloat16)


def draw_queries(key, part):
    key = jax.random.fold_in(key, 2)
    out = jnp.clip(jax.random.normal(key, (TOKENS, QH * HD), jnp.float32), -6.0, 6.0)
    return out.astype(jnp.bfloat16)


def levels(own_key, extent, split, least, high):
    def one(dim, shards_of):
        heights = jax.random.uniform(jax.random.fold_in(jax.random.fold_in(own_key, 6), dim), (shards_of,), jnp.float32, least / len(split), high / len(split))
        return jnp.repeat(jnp.exp(heights), extent[dim] // shards_of).reshape((-1,) + (1,) * (len(extent) - dim - 1))

    gain = one(*split[0])
    for cut in split[1:]:
        gain = gain * one(*cut)
    return gain


def length_profile(amount, total, limit, lean):
    portions = [(1 << 20) // math.isqrt(rank ** lean) + 1 for rank in range(2, amount + 1)]
    spare, given = total - limit - (amount - 1), [1] * (amount - 1)
    while spare > 0:
        candidates = [i for i in range(amount - 1) if given[i] < limit]
        whole, remaining = sum([portions[i] for i in candidates]), spare
        for i in candidates:
            more = min(limit - given[i], max(1, remaining * portions[i] // whole), spare)
            given[i] = given[i] + more
            spare = spare - more
    return np.array([limit] + given)


def uneven_parts(key, amount, total, most, lean):
    if amount == 2:
        one = jax.random.randint(key, (), max(1, total - most), min(most, total - 1) + 1)
        return jnp.stack([one, total - one])
    sizes = jnp.asarray(length_profile(amount, total, most, lean), jnp.int32)
    twos = (amount - 1) // 2
    giver, taker = sizes[1:1 + 2 * twos:2], sizes[2:2 + 2 * twos:2]
    room = jnp.minimum(giver - 1, most - taker)
    passed = jax.random.randint(jax.random.fold_in(key, 1), (twos,), 0, 1 << 20) % (room + 1)
    sizes = sizes.at[1:1 + 2 * twos:2].set(giver - passed).at[2:2 + 2 * twos:2].set(taker + passed)
    return sizes[jax.random.permutation(jax.random.fold_in(key, 2), amount)]


def scatter_about(key, extent, width, limit, shards=(), kind=jnp.bfloat16):
    array = jax.random.normal(key, extent, jnp.float32) * width
    if len(shards) > 0:
        array = levels(key, extent, shards, -0.22, 0.18) * array
    return jnp.clip(array, min=-limit, max=limit).astype(kind)


def setup_inputs(seed: int = 0) -> dict:
    arg_keys = jax.random.split(jax.random.key(seed), 6)
    queries = draw_queries(jax.random.fold_in(arg_keys[5], 71), 0)
    keys = draw_keys(jax.random.fold_in(arg_keys[5], 71), 0)
    values = scatter_about(arg_keys[2], (TOKENS, KVH * HD), 1.0, 6.0, ((0, 512),))
    d_out = scatter_about(arg_keys[3], (TOKENS, QH * HD), 1.0, 6.0, ((0, 512),))
    lengths = uneven_parts(arg_keys[4], DOCS, TOKENS, DOC_MAX, 2).astype(jnp.int32)
    return {"queries": queries, "keys": keys, "values": values, "d_out": d_out, "lengths": lengths}


NEG = -1.0e30


def doc_of(positions, ends):
    return jnp.sum((ends[None, :] <= positions[:, None]).astype(jnp.int32), axis=1)


def reference(queries, keys, values, d_out, lengths):
    rows = TOK_DEV
    reach = (DOC_MAX + rows - 2) // rows
    span = (reach + 1) * rows
    groups = QH // KVH
    scale = HD ** -0.5
    ends = jnp.cumsum(lengths).astype(jnp.int32)
    front = jnp.zeros((reach * rows, KVH * HD), keys.dtype)
    key_pad = jnp.concatenate([front, keys], axis=0)
    value_pad = jnp.concatenate([front, values], axis=0)
    total_rows = TOKENS + reach * rows

    def step(carry, block):
        dk_all, dv_all = carry
        start = (block * rows).astype(jnp.int32)
        query_blk = lax.dynamic_slice_in_dim(queries, start, rows, 0).astype(jnp.float32).reshape(rows, KVH, groups, HD)
        grad_blk = lax.dynamic_slice_in_dim(d_out, start, rows, 0).astype(jnp.float32).reshape(rows, KVH, groups, HD)
        key_win = lax.dynamic_slice_in_dim(key_pad, start, span, 0).astype(jnp.float32).reshape(span, KVH, HD)
        value_win = lax.dynamic_slice_in_dim(value_pad, start, span, 0).astype(jnp.float32).reshape(span, KVH, HD)
        q_pos = start + jnp.arange(rows, dtype=jnp.int32)
        k_pos = start - reach * rows + jnp.arange(span, dtype=jnp.int32)
        allowed = (doc_of(k_pos, ends)[None, :] == doc_of(q_pos, ends)[:, None]) & (k_pos[None, :] <= q_pos[:, None]) & (k_pos[None, :] >= 0)
        score = jnp.einsum('tkgd,skd->kgts', query_blk, key_win) * scale
        score = jnp.where(allowed, score, NEG)
        peak = jnp.max(score, axis=-1)
        lse = peak + jnp.log(jnp.sum(jnp.exp(score - peak[..., None]), axis=-1))
        prob = jnp.where(allowed, jnp.exp(score - lse[..., None]), 0.0)
        prob_b = lax.optimization_barrier(prob.astype(jnp.bfloat16)).astype(jnp.float32)
        attended = jnp.einsum('kgts,skd->tkgd', prob_b, value_win).astype(jnp.bfloat16)
        delta = jnp.sum(attended.astype(jnp.float32) * grad_blk, axis=-1).transpose(1, 2, 0)
        d_prob = jnp.einsum('tkgd,skd->kgts', grad_blk, value_win)
        d_score = lax.optimization_barrier((prob * (d_prob - delta[..., None])).astype(jnp.bfloat16)).astype(jnp.float32)
        d_query = (scale * jnp.einsum('kgts,skd->tkgd', d_score, key_win)).astype(jnp.bfloat16)
        d_key = scale * jnp.einsum('kgts,tkgd->skd', d_score, query_blk)
        d_value = jnp.einsum('kgts,tkgd->skd', prob_b, grad_blk)
        old_k = lax.dynamic_slice_in_dim(dk_all, start, span, 0)
        old_v = lax.dynamic_slice_in_dim(dv_all, start, span, 0)
        dk_all = lax.dynamic_update_slice_in_dim(dk_all, old_k + d_key.reshape(span, KVH * HD), start, 0)
        dv_all = lax.dynamic_update_slice_in_dim(dv_all, old_v + d_value.reshape(span, KVH * HD), start, 0)
        return (dk_all, dv_all), (attended.reshape(rows, QH * HD), d_query.reshape(rows, QH * HD))

    zeros = jnp.zeros((total_rows, KVH * HD), jnp.float32)
    blocks = jnp.arange(TOKENS // rows, dtype=jnp.int32)
    (dk_all, dv_all), (att, dq) = lax.scan(step, (zeros, zeros), blocks)
    attended = att.reshape(TOKENS, QH * HD)
    d_queries = dq.reshape(TOKENS, QH * HD)
    d_keys = dk_all[reach * rows:].astype(jnp.bfloat16)
    d_values = dv_all[reach * rows:].astype(jnp.bfloat16)
    return attended, d_queries, d_keys, d_values
```

```python
import functools
import jax
import jax.numpy as jnp
from jax import lax
from jax.experimental import pallas as pl
from jax.experimental.pallas import tpu as pltpu
from jax.sharding import PartitionSpec as P

QH = 28
KVH = 4
GROUPS = QH // KVH
HD = 128
ROWS = 128
DOCS = 512
AXES = ("ctx", "dp")
NEG = -1e30
SCALE = HD**-0.5
LOG2E = 1.4426950408889634
WIDE = GROUPS * HD

NT = (((1,), (1,)), ((), ()))
NN = (((1,), (0,)), ((), ()))


def dot(a, b, dims):
    return lax.dot_general(a, b, dims, preferred_element_type=jnp.float32)


def shifted(value, steps):
    count = lax.axis_size(AXES)
    leading, last = (max(0, -steps), min(count, count - steps))
    return lax.ppermute(value, AXES, [(source, source + steps) for source in range(leading, last)])


def mask_kernel(start_ref, lengths_ref, bias_ref):
    start = start_ref[0]
    lens = jnp.broadcast_to(lengths_ref[...].astype(jnp.float32), (ROWS, DOCS)).astype(jnp.bfloat16)
    doc = lax.broadcasted_iota(jnp.int32, (DOCS, DOCS), 0)
    upto = lax.broadcasted_iota(jnp.int32, (DOCS, DOCS), 1)
    before = jnp.where(upto <= doc, 1.0, 0.0).astype(jnp.bfloat16)
    ends = dot(before, lens, NT).astype(jnp.int32)
    query = start + lax.broadcasted_iota(jnp.int32, (DOCS, ROWS), 1)
    first = jnp.max(jnp.where(ends <= query, ends, 0), axis=0, keepdims=True)
    first = first - start
    s = lax.broadcasted_iota(jnp.int32, (ROWS, ROWS), 0)
    t = lax.broadcasted_iota(jnp.int32, (ROWS, ROWS), 1)
    merged = jnp.where(s <= t, s, s - 2 * ROWS)
    bias_ref[0:ROWS, :] = jnp.where(merged >= first, 0.0, NEG)
    bias_ref[ROWS:, :] = jnp.where(s - ROWS >= first, 0.0, NEG)


def score_kernel(q_ref, do_ref, ko_ref, vo_ref, kp_ref, vp_ref, kf_ref, vf_ref, bias_ref,
                 prob_ref, ds_ref, near_k_ref, near_v_ref, far_k_ref, far_v_ref):
    def heads(ref):
        return jnp.concatenate([ref[:, h * HD:(h + 1) * HD] for h in range(GROUPS)], axis=0)

    qs = heads(q_ref)
    dos = heads(do_ref)
    s_far = dot(kf_ref[...], qs, NT)
    s_own = dot(ko_ref[...], qs, NT)
    s_near = dot(kp_ref[...], qs, NT)
    d_far = dot(vf_ref[...], dos, NT)
    d_own = dot(vo_ref[...], dos, NT)
    d_near = dot(vp_ref[...], dos, NT)
    tri = (lax.broadcasted_iota(jnp.int32, (ROWS, ROWS), 0)
           <= lax.broadcasted_iota(jnp.int32, (ROWS, ROWS), 1))
    factor = SCALE * LOG2E
    for h in range(GROUPS):
        cols = slice(h * HD, (h + 1) * HD)
        a = jnp.where(tri, s_own[:, cols], s_far[:, cols]) + bias_ref[0:ROWS, :]
        b = s_near[:, cols] + bias_ref[ROWS:, :]
        peak = jnp.max(jnp.maximum(a, b), axis=0, keepdims=True)
        a = jnp.exp2((a - peak) * factor)
        b = jnp.exp2((b - peak) * factor)
        inv = 1.0 / jnp.sum(a + b, axis=0, keepdims=True)
        a = a * inv
        b = b * inv
        da = jnp.where(tri, d_own[:, cols], d_far[:, cols])
        db = d_near[:, cols]
        delta = jnp.sum(a * da + b * db, axis=0, keepdims=True)
        prob_ref[0:ROWS, cols] = a.astype(jnp.bfloat16)
        prob_ref[ROWS:, cols] = b.astype(jnp.bfloat16)
        ds_ref[0:ROWS, cols] = (a * (da - delta)).astype(jnp.bfloat16)
        ds_ref[ROWS:, cols] = (b * (db - delta)).astype(jnp.bfloat16)
    wide_tri = (lax.broadcasted_iota(jnp.int32, (ROWS, WIDE), 0)
                <= lax.broadcasted_iota(jnp.int32, (ROWS, WIDE), 1) % HD)
    none = jnp.zeros((ROWS, WIDE), jnp.bfloat16)
    far_v_ref[...] = dot(jnp.where(wide_tri, none, prob_ref[0:ROWS, :]), dos, NN).astype(jnp.bfloat16)
    near_v_ref[...] = dot(prob_ref[ROWS:, :], dos, NN).astype(jnp.bfloat16)
    far_k_ref[...] = (SCALE * dot(jnp.where(wide_tri, none, ds_ref[0:ROWS, :]), qs, NN)).astype(jnp.bfloat16)
    near_k_ref[...] = (SCALE * dot(ds_ref[ROWS:, :], qs, NN)).astype(jnp.bfloat16)


def finish_kernel(q_ref, do_ref, ko_ref, vo_ref, kp_ref, vp_ref, kf_ref, vf_ref, prob_ref, ds_ref,
                  att_ref, dq_ref, own_k_ref, own_v_ref):
    def heads(ref):
        return jnp.concatenate([ref[:, h * HD:(h + 1) * HD] for h in range(GROUPS)], axis=0)

    qs = heads(q_ref)
    dos = heads(do_ref)
    wide_tri = (lax.broadcasted_iota(jnp.int32, (ROWS, WIDE), 0)
                <= lax.broadcasted_iota(jnp.int32, (ROWS, WIDE), 1) % HD)
    none = jnp.zeros((ROWS, WIDE), jnp.bfloat16)
    p_a = prob_ref[0:ROWS, :]
    p_own = jnp.where(wide_tri, p_a, none)
    p_far = jnp.where(wide_tri, none, p_a)
    ds_a = ds_ref[0:ROWS, :]
    ds_own = jnp.where(wide_tri, ds_a, none)
    ds_far = jnp.where(wide_tri, none, ds_a)
    own_v_ref[...] = dot(p_own, dos, NN)
    own_k_ref[...] = SCALE * dot(ds_own, qs, NN)
    k3 = jnp.concatenate([kf_ref[...], kp_ref[...], ko_ref[...]], axis=0)
    v3 = jnp.concatenate([vf_ref[...], vp_ref[...], vo_ref[...]], axis=0)
    k3t = k3.T
    v3t = v3.T
    p3 = jnp.concatenate([p_far, prob_ref[ROWS:, :], p_own], axis=0)
    ds3 = jnp.concatenate([ds_far, ds_ref[ROWS:, :], ds_own], axis=0)
    att = dot(v3t, p3, NN)
    dq = dot(k3t, ds3, NN) * SCALE
    for h in range(GROUPS):
        cols = slice(h * HD, (h + 1) * HD)
        att_ref[:, cols] = att[:, cols].T.astype(jnp.bfloat16)
        dq_ref[:, cols] = dq[:, cols].T.astype(jnp.bfloat16)


def body(queries, keys, values, d_out, lengths):
    packed = jnp.concatenate([keys, values], axis=1)
    far = shifted(packed, 2)
    near = shifted(packed, 1)
    start = (lax.axis_index(AXES) * ROWS).astype(jnp.int32).reshape(1)
    bias = pl.pallas_call(
        mask_kernel,
        out_shape=jax.ShapeDtypeStruct((2 * ROWS, ROWS), jnp.float32),
        in_specs=[pl.BlockSpec(memory_space=pltpu.SMEM), pl.BlockSpec(memory_space=pltpu.VMEM)],
        out_specs=pl.BlockSpec(memory_space=pltpu.VMEM),
        name="masks",
    )(start, lengths.reshape(1, DOCS))

    head = pl.BlockSpec((ROWS, WIDE), lambda j: (0, j))
    key = pl.BlockSpec((ROWS, HD), lambda j: (0, j))
    value = pl.BlockSpec((ROWS, HD), lambda j: (0, KVH + j))
    square = pl.BlockSpec((None, 2 * ROWS, WIDE), lambda j: (j, 0, 0))
    fixed = pl.BlockSpec((2 * ROWS, ROWS), lambda j: (0, 0))
    term = jax.ShapeDtypeStruct((ROWS, KVH * HD), jnp.bfloat16)
    wide_term = jax.ShapeDtypeStruct((ROWS, KVH * HD), jnp.float32)
    tile = jax.ShapeDtypeStruct((KVH, 2 * ROWS, WIDE), jnp.bfloat16)
    prob, ds, near_k, near_v, far_k, far_v = pl.pallas_call(
        score_kernel,
        grid=(KVH,),
        out_shape=(tile, tile, term, term, term, term),
        in_specs=[head, head, key, key, key, value, key, value, fixed],
        out_specs=(square, square, key, key, key, key),
        name="scores",
        compiler_params=pltpu.CompilerParams(vmem_limit_bytes=32 * 1024 * 1024),
    )(queries, d_out, keys, values, near, near, far, far, bias)
    far_back = shifted(jnp.concatenate([far_k, far_v], axis=1), -2)
    near_back = shifted(jnp.concatenate([near_k, near_v], axis=1), -1)
    attended, d_queries, own_k, own_v = pl.pallas_call(
        finish_kernel,
        grid=(KVH,),
        out_shape=(
            jax.ShapeDtypeStruct((ROWS, QH * HD), jnp.bfloat16),
            jax.ShapeDtypeStruct((ROWS, QH * HD), jnp.bfloat16),
            wide_term,
            wide_term,
        ),
        in_specs=[head, head, key, key, key, value, key, value, square, square],
        out_specs=(head, head, key, key),
        name="finish",
        compiler_params=pltpu.CompilerParams(vmem_limit_bytes=32 * 1024 * 1024),
    )(queries, d_out, keys, values, near, near, far, far, prob, ds)
    cut = KVH * HD
    d_keys = own_k + near_back[:, :cut].astype(jnp.float32) + far_back[:, :cut].astype(jnp.float32)
    d_values = own_v + near_back[:, cut:].astype(jnp.float32) + far_back[:, cut:].astype(jnp.float32)
    return attended, d_queries, d_keys.astype(jnp.bfloat16), d_values.astype(jnp.bfloat16)


def solution(mesh):
    split = P(AXES, None)
    return jax.shard_map(
        body,
        mesh=mesh,
        in_specs=(split, split, split, split, P()),
        out_specs=(split, split, split, split),
        check_vma=False,
    )
```

```python
import jax
import jax.numpy as jnp
from jax import lax
from jax.experimental import pallas as pl
from jax.experimental.pallas import tpu as pltpu
from jax.sharding import PartitionSpec as P

QH = 28
KVH = 4
GROUPS = QH // KVH
HD = 128
ROWS = 128
DOCS = 512
AXES = ("ctx", "dp")
NEG = -1e30
SCALE = HD**-0.5
LOG2E = 1.4426950408889634
WIDE = GROUPS * HD
CUT = KVH * HD

NT = (((1,), (1,)), ((), ()))
NN = (((1,), (0,)), ((), ()))
VMEM = pl.BlockSpec(memory_space=pltpu.VMEM)
SMEM = pl.BlockSpec(memory_space=pltpu.SMEM)
HBM = pl.BlockSpec(memory_space=pltpu.HBM)
ROOM = pltpu.CompilerParams(vmem_limit_bytes=32 * 1024 * 1024)


def dot(a, b, dims):
    return lax.dot_general(a, b, dims, preferred_element_type=jnp.float32)


def shifted(value, steps, every=1):
    count = lax.axis_size(AXES)
    leading, last = (max(0, -steps), min(count, count - steps))
    return lax.ppermute(value, AXES, [(source, source + steps) for source in range(leading, last, every)])


def pinned(value):
    return pltpu.with_memory_space_constraint(value, pltpu.HBM)


def cost(us):
    return pl.CostEstimate(flops=0, bytes_accessed=int(us * 3_000_000), transcendentals=0)


def triangle(width):
    s = lax.broadcasted_iota(jnp.int32, (ROWS, width), 0)
    t = lax.broadcasted_iota(jnp.int32, (ROWS, width), 1) % HD
    return s <= t


def pack_kernel(k_ref, v_ref, out_ref, sems):
    first = pltpu.make_async_copy(k_ref, out_ref.at[0], sems.at[0])
    second = pltpu.make_async_copy(v_ref, out_ref.at[1], sems.at[1])
    first.start()
    second.start()
    first.wait()
    second.wait()


def stage_kernel(start_ref, lengths_ref, q_ref, do_ref, k_ref, v_ref,
                 bias_ref, qs_ref, dos_ref, s_ref, d_ref, kv_ref, len_ref, sems):
    copies = [
        pltpu.make_async_copy(lengths_ref, len_ref, sems.at[0]),
        pltpu.make_async_copy(k_ref, kv_ref.at[0], sems.at[1]),
        pltpu.make_async_copy(v_ref, kv_ref.at[1], sems.at[2]),
    ]
    heads = []
    for j in range(KVH):
        for source, target, sem in ((q_ref, qs_ref, 3 + j), (do_ref, dos_ref, 3 + KVH + j)):
            for h in range(GROUPS):
                column = (j * GROUPS + h) * HD
                heads.append(pltpu.make_async_copy(
                    source.at[:, column:column + HD], target.at[j, h * HD:(h + 1) * HD, :], sems.at[sem]))
    for copy in copies + heads:
        copy.start()
    copies[0].wait()
    start = start_ref[0]
    lens = jnp.broadcast_to(len_ref[...].astype(jnp.float32), (ROWS, DOCS)).astype(jnp.bfloat16)
    doc = lax.broadcasted_iota(jnp.int32, (DOCS, DOCS), 0)
    upto = lax.broadcasted_iota(jnp.int32, (DOCS, DOCS), 1)
    before = jnp.where(upto <= doc, 1.0, 0.0).astype(jnp.bfloat16)
    ends = dot(before, lens, NT).astype(jnp.int32)
    query = start + lax.broadcasted_iota(jnp.int32, (DOCS, ROWS), 1)
    first = jnp.max(jnp.where(ends <= query, ends, 0), axis=0, keepdims=True)
    first = first - start
    s = lax.broadcasted_iota(jnp.int32, (ROWS, ROWS), 0)
    t = lax.broadcasted_iota(jnp.int32, (ROWS, ROWS), 1)
    merged = jnp.where(s <= t, s, s - 2 * ROWS)
    bias_ref[0:ROWS, :] = jnp.where(merged >= first, 0.0, NEG)
    bias_ref[ROWS:, :] = jnp.where(s - ROWS >= first, 0.0, NEG)
    copies[1].wait()
    copies[2].wait()
    for j in range(KVH):
        lanes = slice(j * HD, (j + 1) * HD)
        for h in range(2 * GROUPS):
            heads[2 * GROUPS * j + h].wait()
        s_ref[j] = dot(kv_ref[0, :, lanes], qs_ref[j], NT)
        d_ref[j] = dot(kv_ref[1, :, lanes], dos_ref[j], NT)


def score_kernel(odd_ref, qs_ref, dos_ref, s_ref, d_ref, near_ref, even_far_ref, odd_far_ref, bias_ref,
                 prob_ref, ds_ref, out_ref, far_ref):
    @pl.when(odd_ref[0] == 0)
    def _():
        far_ref[...] = even_far_ref[...]

    @pl.when(odd_ref[0] == 1)
    def _():
        far_ref[...] = odd_far_ref[...]

    tri = triangle(ROWS)
    wide_tri = triangle(WIDE)
    none = jnp.zeros((ROWS, WIDE), jnp.bfloat16)
    factor = SCALE * LOG2E
    for j in range(KVH):
        lanes = slice(j * HD, (j + 1) * HD)
        qs = qs_ref[j]
        dos = dos_ref[j]
        s_far = dot(far_ref[0, :, lanes], qs, NT)
        s_near = dot(near_ref[0, :, lanes], qs, NT)
        d_far = dot(far_ref[1, :, lanes], dos, NT)
        d_near = dot(near_ref[1, :, lanes], dos, NT)
        for h in range(GROUPS):
            cols = slice(h * HD, (h + 1) * HD)
            a = jnp.where(tri, s_ref[j, :, cols], s_far[:, cols]) + bias_ref[0:ROWS, :]
            b = s_near[:, cols] + bias_ref[ROWS:, :]
            peak = jnp.max(jnp.maximum(a, b), axis=0, keepdims=True)
            a = jnp.exp2((a - peak) * factor)
            b = jnp.exp2((b - peak) * factor)
            inv = 1.0 / jnp.sum(a + b, axis=0, keepdims=True)
            a = a * inv
            b = b * inv
            da = jnp.where(tri, d_ref[j, :, cols], d_far[:, cols])
            db = d_near[:, cols]
            delta = jnp.sum(a * da + b * db, axis=0, keepdims=True)
            prob_ref[j, 0:ROWS, cols] = a.astype(jnp.bfloat16)
            prob_ref[j, ROWS:, cols] = b.astype(jnp.bfloat16)
            ds_ref[j, 0:ROWS, cols] = (a * (da - delta)).astype(jnp.bfloat16)
            ds_ref[j, ROWS:, cols] = (b * (db - delta)).astype(jnp.bfloat16)
        out_ref[0, :, lanes] = (
            SCALE * dot(jnp.where(wide_tri, none, ds_ref[j, 0:ROWS, :]), qs, NN)
        ).astype(jnp.bfloat16)
        out_ref[1, :, lanes] = dot(
            jnp.where(wide_tri, none, prob_ref[j, 0:ROWS, :]), dos, NN
        ).astype(jnp.bfloat16)


def near_kernel(odd_ref, qs_ref, dos_ref, prob_ref, ds_ref, passed_ref, out_ref):
    even = odd_ref[0] == 0
    for j in range(KVH):
        lanes = slice(j * HD, (j + 1) * HD)
        key_terms = SCALE * dot(ds_ref[j, ROWS:, :], qs_ref[j], NN)
        value_terms = dot(prob_ref[j, ROWS:, :], dos_ref[j], NN)
        key_terms += jnp.where(even, passed_ref[0, :, lanes].astype(jnp.float32), 0.0)
        value_terms += jnp.where(even, passed_ref[1, :, lanes].astype(jnp.float32), 0.0)
        out_ref[0, :, lanes] = key_terms.astype(jnp.bfloat16)
        out_ref[1, :, lanes] = value_terms.astype(jnp.bfloat16)


def finish_kernel(qs_ref, dos_ref, own_ref, near_ref, far_ref, prob_ref, ds_ref,
                  att_ref, dq_ref, terms_ref):
    wide_tri = triangle(WIDE)
    none = jnp.zeros((ROWS, WIDE), jnp.bfloat16)
    p_a = prob_ref[0:ROWS, :]
    p_own = jnp.where(wide_tri, p_a, none)
    p_far = jnp.where(wide_tri, none, p_a)
    ds_a = ds_ref[0:ROWS, :]
    ds_own = jnp.where(wide_tri, ds_a, none)
    ds_far = jnp.where(wide_tri, none, ds_a)
    terms_ref[0] = SCALE * dot(ds_own, qs_ref[...], NN)
    terms_ref[1] = dot(p_own, dos_ref[...], NN)
    k3t = jnp.concatenate([far_ref[0], near_ref[0], own_ref[0]], axis=0).T
    v3t = jnp.concatenate([far_ref[1], near_ref[1], own_ref[1]], axis=0).T
    p3 = jnp.concatenate([p_far, prob_ref[ROWS:, :], p_own], axis=0)
    ds3 = jnp.concatenate([ds_far, ds_ref[ROWS:, :], ds_own], axis=0)
    att = dot(v3t, p3, NN)
    dq = dot(k3t, ds3, NN) * SCALE
    for h in range(GROUPS):
        cols = slice(h * HD, (h + 1) * HD)
        att_ref[:, cols] = att[:, cols].T.astype(jnp.bfloat16)
        dq_ref[:, cols] = dq[:, cols].T.astype(jnp.bfloat16)


PAIR = jax.ShapeDtypeStruct((2, ROWS, CUT), jnp.bfloat16)
TILE = jax.ShapeDtypeStruct((KVH, 2 * ROWS, WIDE), jnp.bfloat16)
HEAD = pl.BlockSpec((ROWS, WIDE), lambda j: (0, j))
BOTH = pl.BlockSpec((2, ROWS, HD), lambda j: (0, 0, j))
STACK = pl.BlockSpec((None, WIDE, HD), lambda j: (j, 0, 0))
SQUARE = pl.BlockSpec((None, 2 * ROWS, WIDE), lambda j: (j, 0, 0))


def pack(keys, values):
    return pl.pallas_call(
        pack_kernel,
        out_shape=PAIR,
        in_specs=[HBM, HBM],
        out_specs=VMEM,
        scratch_shapes=[pltpu.SemaphoreType.DMA((2,))],
        name="pack",
        compiler_params=ROOM,
    )(pinned(keys), pinned(values))


def stage(start, lengths, queries, d_out, keys, values):
    return pl.pallas_call(
        stage_kernel,
        out_shape=(
            jax.ShapeDtypeStruct((2 * ROWS, ROWS), jnp.float32),
            jax.ShapeDtypeStruct((KVH, WIDE, HD), jnp.bfloat16),
            jax.ShapeDtypeStruct((KVH, WIDE, HD), jnp.bfloat16),
            jax.ShapeDtypeStruct((KVH, ROWS, WIDE), jnp.float32),
            jax.ShapeDtypeStruct((KVH, ROWS, WIDE), jnp.float32),
            PAIR,
        ),
        in_specs=[SMEM] + [HBM] * 5,
        out_specs=(VMEM,) * 6,
        scratch_shapes=[pltpu.VMEM((1, DOCS), jnp.int32), pltpu.SemaphoreType.DMA((3 + 2 * KVH,))],
        name="stage",
        compiler_params=ROOM,
        cost_estimate=cost(3),
    )(start, *(pinned(x) for x in (lengths, queries, d_out, keys, values)))


def scores(odd, qs, dos, s_own, d_own, near, even_far, odd_far, bias):
    return pl.pallas_call(
        score_kernel,
        out_shape=(TILE, TILE, PAIR, PAIR),
        in_specs=[SMEM] + [VMEM] * 8,
        out_specs=(VMEM, VMEM, VMEM, VMEM),
        name="scores",
        compiler_params=ROOM,
        cost_estimate=cost(4),
    )(odd, qs, dos, s_own, d_own, near, even_far, odd_far, bias)


def near_terms(odd, qs, dos, prob, ds, passed):
    return pl.pallas_call(
        near_kernel,
        out_shape=PAIR,
        in_specs=[SMEM] + [VMEM] * 5,
        out_specs=VMEM,
        name="near_terms",
        compiler_params=ROOM,
        cost_estimate=cost(3),
    )(odd, qs, dos, prob, ds, passed)


def finish(qs, dos, own, near, far, prob, ds):
    return pl.pallas_call(
        finish_kernel,
        grid=(KVH,),
        out_shape=(
            jax.ShapeDtypeStruct((ROWS, QH * HD), jnp.bfloat16),
            jax.ShapeDtypeStruct((ROWS, QH * HD), jnp.bfloat16),
            jax.ShapeDtypeStruct((2, ROWS, CUT), jnp.float32),
        ),
        in_specs=[STACK, STACK, BOTH, BOTH, BOTH, SQUARE, SQUARE],
        out_specs=(HEAD, HEAD, BOTH),
        name="finish",
        compiler_params=ROOM,
        cost_estimate=cost(8),
    )(qs, dos, own, near, far, prob, ds)


def body(queries, keys, values, d_out, lengths):
    packed = pack(keys, values)
    near = shifted(packed, 1)
    even_far = shifted(packed, 2, 2)
    index = lax.axis_index(AXES).astype(jnp.int32).reshape(1)
    start = index * ROWS
    odd = index % 2
    bias, qs, dos, s_own, d_own, own = stage(start, lengths.reshape(1, DOCS), queries, d_out, keys, values)
    near, bias = lax.optimization_barrier((near, bias))
    odd_far = shifted(near, 1, 2)
    prob, ds, far_terms, far = scores(odd, qs, dos, s_own, d_own, near, even_far, odd_far, bias)
    passed = shifted(far_terms, -1, 2)
    far_back = shifted(far_terms, -2, 2)
    near_back = shifted(near_terms(odd, qs, dos, prob, ds, passed), -1)
    attended, d_queries, terms = finish(qs, dos, own, near, far, prob, ds)
    d_keys = terms[0] + near_back[0].astype(jnp.float32) + far_back[0].astype(jnp.float32)
    d_values = terms[1] + near_back[1].astype(jnp.float32) + far_back[1].astype(jnp.float32)
    return attended, d_queries, d_keys.astype(jnp.bfloat16), d_values.astype(jnp.bfloat16)


def solution(mesh):
    split = P(AXES, None)
    return jax.shard_map(
        body,
        mesh=mesh,
        in_specs=(split, split, split, split, P()),
        out_specs=(split, split, split, split),
        check_vma=False,
    )
```

```python
import jax
import jax.numpy as jnp
from jax import lax
from jax.experimental import pallas as pl
from jax.experimental.pallas import tpu as pltpu
from jax.sharding import PartitionSpec as P

QH = 28
KVH = 4
GROUPS = QH // KVH
HD = 128
ROWS = 128
DOCS = 512
PARTS = 4
AXES = ("ctx", "dp")
NEG = -1e30
SCALE = HD**-0.5
FACTOR = SCALE * 1.4426950408889634
WIDE = GROUPS * HD
CUT = KVH * HD

NT = (((1,), (1,)), ((), ()))
NN = (((1,), (0,)), ((), ()))
VMEM = pl.BlockSpec(memory_space=pltpu.VMEM)
SMEM = pl.BlockSpec(memory_space=pltpu.SMEM)
HBM = pl.BlockSpec(memory_space=pltpu.HBM)
ROOM = pltpu.CompilerParams(vmem_limit_bytes=32 * 1024 * 1024)


def dot(a, b, dims):
    return lax.dot_general(a, b, dims, preferred_element_type=jnp.float32)


def shifted(value, steps, every=1):
    count = lax.axis_size(AXES)
    leading, last = (max(0, -steps), min(count, count - steps))
    return lax.ppermute(value, AXES, [(source, source + steps) for source in range(leading, last, every)])


def pinned(value):
    return pltpu.with_memory_space_constraint(value, pltpu.HBM)


def cost(us):
    return pl.CostEstimate(flops=0, bytes_accessed=int(us * 3_000_000), transcendentals=0)


def triangle(width):
    s = lax.broadcasted_iota(jnp.int32, (ROWS, width), 0)
    t = lax.broadcasted_iota(jnp.int32, (ROWS, width), 1) % HD
    return s <= t


def pack_kernel(k_ref, v_ref, out_ref, sems):
    copies = []
    for i, ref in enumerate((k_ref, v_ref)):
        for part in range(PARTS):
            rows = slice(part * ROWS // PARTS, (part + 1) * ROWS // PARTS)
            copies.append(pltpu.make_async_copy(ref.at[rows], out_ref.at[i, rows], sems.at[i * PARTS + part]))
    for copy in copies:
        copy.start()
    for copy in copies:
        copy.wait()


def stage_kernel(start_ref, lengths_ref, q_ref, do_ref, k_ref, v_ref,
                 bias_ref, qs_ref, dos_ref, s_ref, d_ref, kv_ref, len_ref, sems):
    copies = [
        pltpu.make_async_copy(lengths_ref, len_ref, sems.at[0]),
        pltpu.make_async_copy(k_ref, kv_ref.at[0], sems.at[1]),
        pltpu.make_async_copy(v_ref, kv_ref.at[1], sems.at[2]),
    ]
    heads = []
    for j in range(KVH):
        for source, target in ((q_ref, qs_ref), (do_ref, dos_ref)):
            for h in range(GROUPS):
                column = (j * GROUPS + h) * HD
                heads.append(pltpu.make_async_copy(
                    source.at[:, column:column + HD], target.at[j, h * HD:(h + 1) * HD, :], sems.at[3 + len(heads)]))
    for copy in copies + heads:
        copy.start()
    copies[0].wait()
    start = start_ref[0]
    lens = jnp.broadcast_to(len_ref[...].astype(jnp.float32), (ROWS, DOCS)).astype(jnp.bfloat16)
    doc = lax.broadcasted_iota(jnp.int32, (DOCS, DOCS), 0)
    upto = lax.broadcasted_iota(jnp.int32, (DOCS, DOCS), 1)
    before = jnp.where(upto <= doc, 1.0, 0.0).astype(jnp.bfloat16)
    ends = dot(before, lens, NT).astype(jnp.int32)
    query = start + lax.broadcasted_iota(jnp.int32, (DOCS, ROWS), 1)
    first = jnp.max(jnp.where(ends <= query, ends, 0), axis=0, keepdims=True)
    first = first - start
    s = lax.broadcasted_iota(jnp.int32, (ROWS, ROWS), 0)
    t = lax.broadcasted_iota(jnp.int32, (ROWS, ROWS), 1)
    merged = jnp.where(s <= t, s, s - 2 * ROWS)
    bias_ref[0:ROWS, :] = jnp.where(merged >= first, 0.0, NEG)
    bias_ref[ROWS:, :] = jnp.where(s - ROWS >= first, 0.0, NEG)
    copies[1].wait()
    copies[2].wait()
    for j in range(KVH):
        lanes = slice(j * HD, (j + 1) * HD)
        for h in range(2 * GROUPS):
            heads[2 * GROUPS * j + h].wait()
        s_ref[j] = dot(kv_ref[0, :, lanes], qs_ref[j], NT) * FACTOR
        d_ref[j] = dot(kv_ref[1, :, lanes], dos_ref[j], NT)


def near_score_kernel(qs_ref, dos_ref, near_ref, bias_ref, s_ref, d_ref):
    for j in range(KVH):
        lanes = slice(j * HD, (j + 1) * HD)
        s = dot(near_ref[0, :, lanes], qs_ref[j], NT)
        for h in range(GROUPS):
            cols = slice(h * HD, (h + 1) * HD)
            s_ref[j, :, cols] = s[:, cols] * FACTOR + bias_ref[ROWS:, :]
        d_ref[j] = dot(near_ref[1, :, lanes], dos_ref[j], NT)


def score_kernel(odd_ref, qs_ref, dos_ref, so_ref, do_ref, sn_ref, dn_ref, even_far_ref, odd_far_ref, bias_ref,
                 prob_ref, ds_ref, out_ref, far_ref):
    odd = odd_ref[0] == 1
    far_ref[...] = jnp.where(odd, odd_far_ref[...], even_far_ref[...])
    tri = triangle(ROWS)
    wide_tri = triangle(WIDE)
    none = jnp.zeros((ROWS, WIDE), jnp.bfloat16)
    for j in range(KVH):
        lanes = slice(j * HD, (j + 1) * HD)
        s_far = dot(far_ref[0, :, lanes], qs_ref[j], NT)
        d_far = dot(far_ref[1, :, lanes], dos_ref[j], NT)
        for h in range(GROUPS):
            cols = slice(h * HD, (h + 1) * HD)
            a = jnp.where(tri, so_ref[j, :, cols], s_far[:, cols] * FACTOR) + bias_ref[0:ROWS, :]
            b = sn_ref[j, :, cols]
            peak = jnp.max(jnp.maximum(a, b), axis=0, keepdims=True)
            a = jnp.exp2(a - peak)
            b = jnp.exp2(b - peak)
            inv = 1.0 / jnp.sum(a + b, axis=0, keepdims=True)
            a = a * inv
            b = b * inv
            da = jnp.where(tri, do_ref[j, :, cols], d_far[:, cols])
            db = dn_ref[j, :, cols]
            delta = jnp.sum(a * da + b * db, axis=0, keepdims=True)
            prob_ref[j, 0:ROWS, cols] = a.astype(jnp.bfloat16)
            prob_ref[j, ROWS:, cols] = b.astype(jnp.bfloat16)
            ds_ref[j, 0:ROWS, cols] = (a * (da - delta)).astype(jnp.bfloat16)
            ds_ref[j, ROWS:, cols] = (b * (db - delta)).astype(jnp.bfloat16)
    for j in range(KVH):
        lanes = slice(j * HD, (j + 1) * HD)
        out_ref[0, :, lanes] = (
            SCALE * dot(jnp.where(wide_tri, none, ds_ref[j, 0:ROWS, :]), qs_ref[j], NN)
        ).astype(jnp.bfloat16)
        out_ref[1, :, lanes] = dot(
            jnp.where(wide_tri, none, prob_ref[j, 0:ROWS, :]), dos_ref[j], NN
        ).astype(jnp.bfloat16)


def near_kernel(odd_ref, qs_ref, dos_ref, prob_ref, ds_ref, passed_ref, out_ref):
    even = odd_ref[0] == 0
    for j in range(KVH):
        lanes = slice(j * HD, (j + 1) * HD)
        key_terms = SCALE * dot(ds_ref[j, ROWS:, :], qs_ref[j], NN)
        value_terms = dot(prob_ref[j, ROWS:, :], dos_ref[j], NN)
        key_terms += jnp.where(even, passed_ref[0, :, lanes].astype(jnp.float32), 0.0)
        value_terms += jnp.where(even, passed_ref[1, :, lanes].astype(jnp.float32), 0.0)
        out_ref[0, :, lanes] = key_terms.astype(jnp.bfloat16)
        out_ref[1, :, lanes] = value_terms.astype(jnp.bfloat16)


def finish_kernel(qs_ref, dos_ref, own_ref, near_ref, far_ref, prob_ref, ds_ref,
                  att_ref, dq_ref, terms_ref):
    wide_tri = triangle(WIDE)
    none = jnp.zeros((ROWS, WIDE), jnp.bfloat16)
    p_a = prob_ref[0:ROWS, :]
    p_own = jnp.where(wide_tri, p_a, none)
    p_far = jnp.where(wide_tri, none, p_a)
    ds_a = ds_ref[0:ROWS, :]
    ds_own = jnp.where(wide_tri, ds_a, none)
    ds_far = jnp.where(wide_tri, none, ds_a)
    terms_ref[0] = SCALE * dot(ds_own, qs_ref[...], NN)
    terms_ref[1] = dot(p_own, dos_ref[...], NN)
    k3t = jnp.concatenate([far_ref[0], near_ref[0], own_ref[0]], axis=0).T
    v3t = jnp.concatenate([far_ref[1], near_ref[1], own_ref[1]], axis=0).T
    p3 = jnp.concatenate([p_far, prob_ref[ROWS:, :], p_own], axis=0)
    ds3 = jnp.concatenate([ds_far, ds_ref[ROWS:, :], ds_own], axis=0)
    att = dot(v3t, p3, NN)
    dq = dot(k3t, ds3, NN) * SCALE
    for h in range(GROUPS):
        cols = slice(h * HD, (h + 1) * HD)
        att_ref[:, cols] = att[:, cols].T.astype(jnp.bfloat16)
        dq_ref[:, cols] = dq[:, cols].T.astype(jnp.bfloat16)


PAIR = jax.ShapeDtypeStruct((2, ROWS, CUT), jnp.bfloat16)
SCORE = jax.ShapeDtypeStruct((KVH, ROWS, WIDE), jnp.float32)
TILE = jax.ShapeDtypeStruct((KVH, 2 * ROWS, WIDE), jnp.bfloat16)
HEAD = pl.BlockSpec((ROWS, WIDE), lambda j: (0, j))
BOTH = pl.BlockSpec((2, ROWS, HD), lambda j: (0, 0, j))
STACK = pl.BlockSpec((None, WIDE, HD), lambda j: (j, 0, 0))
SQUARE = pl.BlockSpec((None, 2 * ROWS, WIDE), lambda j: (j, 0, 0))


def pack(keys, values):
    return pl.pallas_call(
        pack_kernel,
        out_shape=PAIR,
        in_specs=[HBM, HBM],
        out_specs=VMEM,
        scratch_shapes=[pltpu.SemaphoreType.DMA((2 * PARTS,))],
        name="pack",
        compiler_params=ROOM,
    )(pinned(keys), pinned(values))


def stage(start, lengths, queries, d_out, keys, values):
    return pl.pallas_call(
        stage_kernel,
        out_shape=(
            jax.ShapeDtypeStruct((2 * ROWS, ROWS), jnp.float32),
            jax.ShapeDtypeStruct((KVH, WIDE, HD), jnp.bfloat16),
            jax.ShapeDtypeStruct((KVH, WIDE, HD), jnp.bfloat16),
            SCORE,
            SCORE,
            PAIR,
        ),
        in_specs=[SMEM] + [HBM] * 5,
        out_specs=(VMEM,) * 6,
        scratch_shapes=[pltpu.VMEM((1, DOCS), jnp.int32), pltpu.SemaphoreType.DMA((3 + 2 * QH,))],
        name="stage",
        compiler_params=ROOM,
        cost_estimate=cost(3),
    )(start, *(pinned(x) for x in (lengths, queries, d_out, keys, values)))


def near_scores(qs, dos, near, bias):
    return pl.pallas_call(
        near_score_kernel,
        out_shape=(SCORE, SCORE),
        in_specs=[VMEM] * 4,
        out_specs=(VMEM, VMEM),
        name="near_scores",
        compiler_params=ROOM,
        cost_estimate=cost(2),
    )(qs, dos, near, bias)


def scores(odd, qs, dos, s_own, d_own, s_near, d_near, even_far, odd_far, bias):
    return pl.pallas_call(
        score_kernel,
        out_shape=(TILE, TILE, PAIR, PAIR),
        in_specs=[SMEM] + [VMEM] * 9,
        out_specs=(VMEM, VMEM, VMEM, VMEM),
        name="scores",
        compiler_params=ROOM,
        cost_estimate=cost(4),
    )(odd, qs, dos, s_own, d_own, s_near, d_near, even_far, odd_far, bias)


def near_terms(odd, qs, dos, prob, ds, passed):
    return pl.pallas_call(
        near_kernel,
        out_shape=PAIR,
        in_specs=[SMEM] + [VMEM] * 5,
        out_specs=VMEM,
        name="near_terms",
        compiler_params=ROOM,
        cost_estimate=cost(3),
    )(odd, qs, dos, prob, ds, passed)


def finish(qs, dos, own, near, far, prob, ds):
    return pl.pallas_call(
        finish_kernel,
        grid=(KVH,),
        out_shape=(
            jax.ShapeDtypeStruct((ROWS, QH * HD), jnp.bfloat16),
            jax.ShapeDtypeStruct((ROWS, QH * HD), jnp.bfloat16),
            jax.ShapeDtypeStruct((2, ROWS, CUT), jnp.float32),
        ),
        in_specs=[STACK, STACK, BOTH, BOTH, BOTH, SQUARE, SQUARE],
        out_specs=(HEAD, HEAD, BOTH),
        name="finish",
        compiler_params=ROOM,
        cost_estimate=cost(8),
    )(qs, dos, own, near, far, prob, ds)


def body(queries, keys, values, d_out, lengths):
    packed = pack(keys, values)
    near = shifted(packed, 1)
    even_far = shifted(packed, 2, 2)
    index = lax.axis_index(AXES).astype(jnp.int32).reshape(1)
    start = index * ROWS
    odd = index % 2
    bias, qs, dos, s_own, d_own, own = stage(start, lengths.reshape(1, DOCS), queries, d_out, keys, values)
    near, bias = lax.optimization_barrier((near, bias))
    odd_far = shifted(near, 1, 2)
    s_near, d_near = near_scores(qs, dos, near, bias)
    prob, ds, far_terms, far = scores(odd, qs, dos, s_own, d_own, s_near, d_near, even_far, odd_far, bias)
    passed = shifted(far_terms, -1, 2)
    far_back = shifted(far_terms, -2, 2)
    near_back = shifted(near_terms(odd, qs, dos, prob, ds, passed), -1)
    attended, d_queries, terms = finish(qs, dos, own, near, far, prob, ds)
    d_keys = terms[0] + near_back[0].astype(jnp.float32) + far_back[0].astype(jnp.float32)
    d_values = terms[1] + near_back[1].astype(jnp.float32) + far_back[1].astype(jnp.float32)
    return attended, d_queries, d_keys.astype(jnp.bfloat16), d_values.astype(jnp.bfloat16)


def solution(mesh):
    split = P(AXES, None)
    return jax.shard_map(
        body,
        mesh=mesh,
        in_specs=(split, split, split, split, P()),
        out_specs=(split, split, split, split),
        check_vma=False,
    )
```

```python
import jax
import jax.numpy as jnp
from jax import lax
from jax.experimental import pallas as pl
from jax.experimental.pallas import tpu as pltpu
from jax.sharding import PartitionSpec as P

QH = 28
KVH = 4
GROUPS = QH // KVH
HD = 128
ROWS = 128
DOCS = 512
PARTS = 4
AXES = ("ctx", "dp")
NEG = -1e30
SCALE = HD**-0.5
FACTOR = SCALE * 1.4426950408889634
WIDE = GROUPS * HD
CUT = KVH * HD

NT = (((1,), (1,)), ((), ()))
NN = (((1,), (0,)), ((), ()))
VMEM = pl.BlockSpec(memory_space=pltpu.VMEM)
SMEM = pl.BlockSpec(memory_space=pltpu.SMEM)
HBM = pl.BlockSpec(memory_space=pltpu.HBM)
ROOM = pltpu.CompilerParams(vmem_limit_bytes=32 * 1024 * 1024)


def dot(a, b, dims):
    return lax.dot_general(a, b, dims, preferred_element_type=jnp.float32)


def shifted(value, steps, every=1):
    count = lax.axis_size(AXES)
    leading, last = (max(0, -steps), min(count, count - steps))
    return lax.ppermute(value, AXES, [(source, source + steps) for source in range(leading, last, every)])


def pinned(value):
    return pltpu.with_memory_space_constraint(value, pltpu.HBM)


def cost(us):
    return pl.CostEstimate(flops=0, bytes_accessed=int(us * 3_000_000), transcendentals=0)


def triangle(width):
    s = lax.broadcasted_iota(jnp.int32, (ROWS, width), 0)
    t = lax.broadcasted_iota(jnp.int32, (ROWS, width), 1) % HD
    return s <= t


def pack_kernel(k_ref, v_ref, lengths_ref, out_ref, len_ref, sems):
    copies = [pltpu.make_async_copy(lengths_ref, len_ref, sems.at[2 * PARTS])]
    for i, ref in enumerate((k_ref, v_ref)):
        for part in range(PARTS):
            rows = slice(part * ROWS // PARTS, (part + 1) * ROWS // PARTS)
            copies.append(pltpu.make_async_copy(ref.at[rows], out_ref.at[i, rows], sems.at[i * PARTS + part]))
    for copy in copies:
        copy.start()
    for copy in copies:
        copy.wait()


def heads(ref, j):
    first = j * GROUPS
    return jnp.concatenate([ref[:, h * HD:(h + 1) * HD] for h in range(first, first + GROUPS)], axis=0)


def down(fold, x):
    return fold(x, axis=0, keepdims=True)


def stage_kernel(start_ref, len_ref, q_in, do_in, kv_ref,
                 bias_ref, q_ref, do_ref, e_ref, d_ref, stat_ref, sems):
    copies = []
    for i, wide in enumerate((slice(0, WIDE), slice(WIDE, KVH * WIDE))):
        copies.append(pltpu.make_async_copy(q_in.at[:, wide], q_ref.at[:, wide], sems.at[2 * i]))
        copies.append(pltpu.make_async_copy(do_in.at[:, wide], do_ref.at[:, wide], sems.at[2 * i + 1]))
    for copy in copies:
        copy.start()
    start = start_ref[0]
    lens = jnp.broadcast_to(len_ref[...].astype(jnp.float32), (ROWS, DOCS)).astype(jnp.bfloat16)
    doc = lax.broadcasted_iota(jnp.int32, (DOCS, DOCS), 0)
    upto = lax.broadcasted_iota(jnp.int32, (DOCS, DOCS), 1)
    before = jnp.where(upto <= doc, 1.0, 0.0).astype(jnp.bfloat16)
    ends = dot(before, lens, NT).astype(jnp.int32)
    query = start + lax.broadcasted_iota(jnp.int32, (DOCS, ROWS), 1)
    first = down(jnp.max, jnp.where(ends <= query, ends, 0)) - start
    s = lax.broadcasted_iota(jnp.int32, (ROWS, ROWS), 0)
    t = lax.broadcasted_iota(jnp.int32, (ROWS, ROWS), 1)
    own_bias = jnp.where((s <= t) & (s >= first), 0.0, NEG)
    bias_ref[0] = jnp.where((s > t) & (s - 2 * ROWS >= first), 0.0, NEG)
    bias_ref[1] = jnp.where(s - ROWS >= first, 0.0, NEG)
    for j in range(KVH):
        lanes = slice(j * HD, (j + 1) * HD)
        if j < 2:
            copies[2 * j].wait()
            copies[2 * j + 1].wait()
        score = dot(kv_ref[0, :, lanes], heads(q_ref, j), NT)
        d_prob = dot(kv_ref[1, :, lanes], heads(do_ref, j), NT)
        for h in range(GROUPS):
            cols = slice(h * HD, (h + 1) * HD)
            x = score[:, cols] * FACTOR + own_bias
            peak = down(jnp.max, x)
            e = jnp.exp2(x - peak)
            e_ref[j, :, cols] = e
            d_ref[j, :, cols] = d_prob[:, cols]
            stat_ref[j, 0:1, cols] = peak
            stat_ref[j, 1:2, cols] = down(jnp.sum, e)
            stat_ref[j, 2:3, cols] = down(jnp.sum, e * d_prob[:, cols])


def near_score_kernel(q_ref, do_ref, near_ref, bias_ref, stat_ref, e_ref, d_ref, out_ref):
    for j in range(KVH):
        lanes = slice(j * HD, (j + 1) * HD)
        score = dot(near_ref[0, :, lanes], heads(q_ref, j), NT)
        d_prob = dot(near_ref[1, :, lanes], heads(do_ref, j), NT)
        for h in range(GROUPS):
            cols = slice(h * HD, (h + 1) * HD)
            x = score[:, cols] * FACTOR + bias_ref[1]
            peak = jnp.maximum(stat_ref[j, 0:1, cols], down(jnp.max, x))
            own = jnp.exp2(stat_ref[j, 0:1, cols] - peak)
            e = jnp.exp2(x - peak)
            e_ref[j, :, cols] = e
            d_ref[j, :, cols] = d_prob[:, cols]
            out_ref[j, 0:1, cols] = peak
            out_ref[j, 1:2, cols] = stat_ref[j, 1:2, cols] * own + down(jnp.sum, e)
            out_ref[j, 2:3, cols] = stat_ref[j, 2:3, cols] * own + down(jnp.sum, e * d_prob[:, cols])
            out_ref[j, 3:4, cols] = own


def score_kernel(odd_ref, q_ref, do_ref, e_ref, d_ref, stat_ref, even_far_ref, odd_far_ref, bias_ref,
                 prob_ref, ds_ref, terms_ref, far_ref, out_ref):
    odd = odd_ref[0] == 1
    far_ref[...] = jnp.where(odd, odd_far_ref[...], even_far_ref[...])
    for j in range(KVH):
        lanes = slice(j * HD, (j + 1) * HD)
        score = dot(far_ref[0, :, lanes], heads(q_ref, j), NT)
        d_prob = dot(far_ref[1, :, lanes], heads(do_ref, j), NT)
        for h in range(GROUPS):
            cols = slice(h * HD, (h + 1) * HD)
            x = score[:, cols] * FACTOR + bias_ref[0]
            peak = jnp.maximum(stat_ref[j, 0:1, cols], down(jnp.max, x))
            old = jnp.exp2(stat_ref[j, 0:1, cols] - peak)
            e = jnp.exp2(x - peak)
            inv = 1.0 / (stat_ref[j, 1:2, cols] * old + down(jnp.sum, e))
            delta = (stat_ref[j, 2:3, cols] * old + down(jnp.sum, e * d_prob[:, cols])) * inv
            a = e * inv
            b = e_ref[j, :, cols] * (old * inv)
            prob_ref[j, 0:ROWS, cols] = a.astype(jnp.bfloat16)
            prob_ref[j, ROWS:, cols] = b.astype(jnp.bfloat16)
            ds_ref[j, 0:ROWS, cols] = (a * (d_prob[:, cols] - delta)).astype(jnp.bfloat16)
            ds_ref[j, ROWS:, cols] = (b * (d_ref[j, :, cols] - delta)).astype(jnp.bfloat16)
            out_ref[j, 0:1, cols] = stat_ref[j, 3:4, cols] * old * inv
            out_ref[j, 1:2, cols] = delta
    for j in range(KVH):
        lanes = slice(j * HD, (j + 1) * HD)
        terms_ref[0, :, lanes] = (SCALE * dot(ds_ref[j, 0:ROWS, :], heads(q_ref, j), NN)).astype(jnp.bfloat16)
        terms_ref[1, :, lanes] = dot(prob_ref[j, 0:ROWS, :], heads(do_ref, j), NN).astype(jnp.bfloat16)


def near_kernel(odd_ref, q_ref, do_ref, prob_ref, ds_ref, passed_ref, out_ref):
    even = odd_ref[0] == 0
    for j in range(KVH):
        lanes = slice(j * HD, (j + 1) * HD)
        key_terms = SCALE * dot(ds_ref[j, ROWS:, :], heads(q_ref, j), NN)
        value_terms = dot(prob_ref[j, ROWS:, :], heads(do_ref, j), NN)
        key_terms += jnp.where(even, passed_ref[0, :, lanes].astype(jnp.float32), 0.0)
        value_terms += jnp.where(even, passed_ref[1, :, lanes].astype(jnp.float32), 0.0)
        out_ref[0, :, lanes] = key_terms.astype(jnp.bfloat16)
        out_ref[1, :, lanes] = value_terms.astype(jnp.bfloat16)


def finish_kernel(q_ref, do_ref, own_ref, near_ref, far_ref, prob_ref, ds_ref, e_ref, d_ref, stat_ref,
                  att_ref, dq_ref, terms_ref):
    p_own = e_ref[...] * stat_ref[0:1, :]
    ds_own = (p_own * (d_ref[...] - stat_ref[1:2, :])).astype(jnp.bfloat16)
    p_own = p_own.astype(jnp.bfloat16)
    terms_ref[0] = SCALE * dot(ds_own, heads(q_ref, 0), NN)
    terms_ref[1] = dot(p_own, heads(do_ref, 0), NN)
    k3t = jnp.concatenate([far_ref[0], near_ref[0], own_ref[0]], axis=0).T
    v3t = jnp.concatenate([far_ref[1], near_ref[1], own_ref[1]], axis=0).T
    p3 = jnp.concatenate([prob_ref[...], p_own], axis=0)
    ds3 = jnp.concatenate([ds_ref[...], ds_own], axis=0)
    att = dot(v3t, p3, NN)
    dq = dot(k3t, ds3, NN) * SCALE
    for h in range(GROUPS):
        cols = slice(h * HD, (h + 1) * HD)
        att_ref[:, cols] = att[:, cols].T.astype(jnp.bfloat16)
        dq_ref[:, cols] = dq[:, cols].T.astype(jnp.bfloat16)


PAIR = jax.ShapeDtypeStruct((2, ROWS, CUT), jnp.bfloat16)
FULL = jax.ShapeDtypeStruct((ROWS, QH * HD), jnp.bfloat16)
SCORE = jax.ShapeDtypeStruct((KVH, ROWS, WIDE), jnp.float32)
TILE = jax.ShapeDtypeStruct((KVH, 2 * ROWS, WIDE), jnp.bfloat16)
STAT = jax.ShapeDtypeStruct((KVH, 8, WIDE), jnp.float32)
HEAD = pl.BlockSpec((ROWS, WIDE), lambda j: (0, j))
BOTH = pl.BlockSpec((2, ROWS, HD), lambda j: (0, 0, j))
SQUARE = pl.BlockSpec((None, 2 * ROWS, WIDE), lambda j: (j, 0, 0))
LINE = pl.BlockSpec((None, ROWS, WIDE), lambda j: (j, 0, 0))
FEW = pl.BlockSpec((None, 8, WIDE), lambda j: (j, 0, 0))


def pack(keys, values, lengths):
    return pl.pallas_call(
        pack_kernel,
        out_shape=(PAIR, jax.ShapeDtypeStruct((1, DOCS), jnp.int32)),
        in_specs=[HBM] * 3,
        out_specs=(VMEM, VMEM),
        scratch_shapes=[pltpu.SemaphoreType.DMA((2 * PARTS + 1,))],
        name="pack",
        compiler_params=ROOM,
    )(pinned(keys), pinned(values), pinned(lengths))


def stage(start, lengths, queries, d_out, own):
    return pl.pallas_call(
        stage_kernel,
        out_shape=(jax.ShapeDtypeStruct((2, ROWS, ROWS), jnp.float32), FULL, FULL, SCORE, SCORE, STAT),
        in_specs=[SMEM, VMEM, HBM, HBM, VMEM],
        out_specs=(VMEM,) * 6,
        scratch_shapes=[pltpu.SemaphoreType.DMA((4,))],
        name="stage",
        compiler_params=ROOM,
        cost_estimate=cost(3),
    )(start, lengths, pinned(queries), pinned(d_out), own)


def near_scores(q, do, near, bias, stat):
    return pl.pallas_call(
        near_score_kernel,
        out_shape=(SCORE, SCORE, STAT),
        in_specs=[VMEM] * 5,
        out_specs=(VMEM,) * 3,
        name="near_scores",
        compiler_params=ROOM,
        cost_estimate=cost(2),
    )(q, do, near, bias, stat)


def scores(odd, q, do, e_near, d_near, stat, even_far, odd_far, bias):
    return pl.pallas_call(
        score_kernel,
        out_shape=(TILE, TILE, PAIR, PAIR, STAT),
        in_specs=[SMEM] + [VMEM] * 8,
        out_specs=(VMEM,) * 5,
        name="scores",
        compiler_params=ROOM,
        cost_estimate=cost(4),
    )(odd, q, do, e_near, d_near, stat, even_far, odd_far, bias)


def near_terms(odd, q, do, prob, ds, passed):
    return pl.pallas_call(
        near_kernel,
        out_shape=PAIR,
        in_specs=[SMEM] + [VMEM] * 5,
        out_specs=VMEM,
        name="near_terms",
        compiler_params=ROOM,
        cost_estimate=cost(3),
    )(odd, q, do, prob, ds, passed)


def finish(q, do, own, near, far, prob, ds, e_own, d_own, stat):
    return pl.pallas_call(
        finish_kernel,
        grid=(KVH,),
        out_shape=(FULL, FULL, jax.ShapeDtypeStruct((2, ROWS, CUT), jnp.float32)),
        in_specs=[HEAD, HEAD, BOTH, BOTH, BOTH, SQUARE, SQUARE, LINE, LINE, FEW],
        out_specs=(HEAD, HEAD, BOTH),
        name="finish",
        compiler_params=ROOM,
        cost_estimate=cost(8),
    )(q, do, own, near, far, prob, ds, e_own, d_own, stat)


def body(queries, keys, values, d_out, lengths):
    own, lens = pack(keys, values, lengths.reshape(1, DOCS))
    near = shifted(own, 1)
    even_far = shifted(own, 2, 2)
    index = lax.axis_index(AXES).astype(jnp.int32).reshape(1)
    start = index * ROWS
    odd = index % 2
    bias, q, do, e_own, d_own, stat = stage(start, lens, queries, d_out, own)
    near, bias = lax.optimization_barrier((near, bias))
    odd_far = shifted(near, 1, 2)
    e_near, d_near, stat = near_scores(q, do, near, bias, stat)
    prob, ds, far_terms, far, stat = scores(odd, q, do, e_near, d_near, stat, even_far, odd_far, bias)
    passed = shifted(far_terms, -1, 2)
    far_back = shifted(far_terms, -2, 2)
    near_back = shifted(near_terms(odd, q, do, prob, ds, passed), -1)
    attended, d_queries, terms = finish(q, do, own, near, far, prob, ds, e_own, d_own, stat)
    d_keys = terms[0] + near_back[0].astype(jnp.float32) + far_back[0].astype(jnp.float32)
    d_values = terms[1] + near_back[1].astype(jnp.float32) + far_back[1].astype(jnp.float32)
    return attended, d_queries, d_keys.astype(jnp.bfloat16), d_values.astype(jnp.bfloat16)


def solution(mesh):
    split = P(AXES, None)
    return jax.shard_map(
        body,
        mesh=mesh,
        in_specs=(split, split, split, split, P()),
        out_specs=(split, split, split, split),
        check_vma=False,
    )
```

```python
import jax
import jax.numpy as jnp
from jax import lax
from jax.experimental import pallas as pl
from jax.experimental.pallas import tpu as pltpu
from jax.sharding import PartitionSpec as P

QH = 28
KVH = 4
GROUPS = QH // KVH
HD = 128
ROWS = 128
DOCS = 512
PARTS = 4
AXES = ("ctx", "dp")
NEG = -1e30
SCALE = HD**-0.5
FACTOR = SCALE * 1.4426950408889634
WIDE = GROUPS * HD
CUT = KVH * HD

NT = (((1,), (1,)), ((), ()))
NN = (((1,), (0,)), ((), ()))
VMEM = pl.BlockSpec(memory_space=pltpu.VMEM)
SMEM = pl.BlockSpec(memory_space=pltpu.SMEM)
HBM = pl.BlockSpec(memory_space=pltpu.HBM)
ROOM = pltpu.CompilerParams(vmem_limit_bytes=32 * 1024 * 1024)


def dot(a, b, dims):
    return lax.dot_general(a, b, dims, preferred_element_type=jnp.float32)


def shifted(value, steps, every=1):
    count = lax.axis_size(AXES)
    leading, last = (max(0, -steps), min(count, count - steps))
    return lax.ppermute(value, AXES, [(source, source + steps) for source in range(leading, last, every)])


def pinned(value):
    return pltpu.with_memory_space_constraint(value, pltpu.HBM)


def cost(us):
    return pl.CostEstimate(flops=0, bytes_accessed=int(us * 3_000_000), transcendentals=0)


def triangle(width):
    s = lax.broadcasted_iota(jnp.int32, (ROWS, width), 0)
    t = lax.broadcasted_iota(jnp.int32, (ROWS, width), 1) % HD
    return s <= t


def pack_kernel(k_ref, v_ref, lengths_ref, out_ref, len_ref, sems):
    copies = [pltpu.make_async_copy(lengths_ref, len_ref, sems.at[2 * PARTS])]
    for i, ref in enumerate((k_ref, v_ref)):
        for part in range(PARTS):
            rows = slice(part * ROWS // PARTS, (part + 1) * ROWS // PARTS)
            copies.append(pltpu.make_async_copy(ref.at[rows], out_ref.at[i, rows], sems.at[i * PARTS + part]))
    for copy in copies:
        copy.start()
    for copy in copies:
        copy.wait()


def heads(ref, j):
    first = j * GROUPS
    return jnp.concatenate([ref[:, h * HD:(h + 1) * HD] for h in range(first, first + GROUPS)], axis=0)


def down(fold, x):
    return fold(x, axis=0, keepdims=True)


def stage_kernel(start_ref, len_ref, q_in, do_in, kv_ref,
                 bias_ref, q_ref, do_ref, e_ref, d_ref, stat_ref, sems):
    copies = []
    for i, wide in enumerate((slice(0, WIDE), slice(WIDE, KVH * WIDE))):
        copies.append(pltpu.make_async_copy(q_in.at[:, wide], q_ref.at[:, wide], sems.at[2 * i]))
        copies.append(pltpu.make_async_copy(do_in.at[:, wide], do_ref.at[:, wide], sems.at[2 * i + 1]))
    for copy in copies:
        copy.start()
    start = start_ref[0]
    lens = jnp.broadcast_to(len_ref[...].astype(jnp.float32), (ROWS, DOCS)).astype(jnp.bfloat16)
    doc = lax.broadcasted_iota(jnp.int32, (DOCS, DOCS), 0)
    upto = lax.broadcasted_iota(jnp.int32, (DOCS, DOCS), 1)
    before = jnp.where(upto <= doc, 1.0, 0.0).astype(jnp.bfloat16)
    ends = dot(before, lens, NT).astype(jnp.int32)
    query = start + lax.broadcasted_iota(jnp.int32, (DOCS, ROWS), 1)
    first = down(jnp.max, jnp.where(ends <= query, ends, 0)) - start
    s = lax.broadcasted_iota(jnp.int32, (ROWS, ROWS), 0)
    t = lax.broadcasted_iota(jnp.int32, (ROWS, ROWS), 1)
    own_bias = jnp.where((s <= t) & (s >= first), 0.0, NEG)
    bias_ref[0] = jnp.where((s > t) & (s - 2 * ROWS >= first), 0.0, NEG)
    bias_ref[1] = jnp.where(s - ROWS >= first, 0.0, NEG)
    for j in range(KVH):
        lanes = slice(j * HD, (j + 1) * HD)
        if j < 2:
            copies[2 * j].wait()
            copies[2 * j + 1].wait()
        score = dot(kv_ref[0, :, lanes], heads(q_ref, j), NT)
        d_prob = dot(kv_ref[1, :, lanes], heads(do_ref, j), NT)
        for h in range(GROUPS):
            cols = slice(h * HD, (h + 1) * HD)
            x = score[:, cols] * FACTOR + own_bias
            peak = down(jnp.max, x)
            e = jnp.exp2(x - peak)
            e_ref[j, :, cols] = e
            d_ref[j, :, cols] = d_prob[:, cols]
            stat_ref[j, 0:1, cols] = peak
            stat_ref[j, 1:2, cols] = down(jnp.sum, e)
            stat_ref[j, 2:3, cols] = down(jnp.sum, e * d_prob[:, cols])


def near_score_kernel(q_ref, do_ref, near_ref, bias_ref, stat_ref, e_ref, d_ref, out_ref):
    for j in range(KVH):
        lanes = slice(j * HD, (j + 1) * HD)
        score = dot(near_ref[0, :, lanes], heads(q_ref, j), NT)
        d_prob = dot(near_ref[1, :, lanes], heads(do_ref, j), NT)
        for h in range(GROUPS):
            cols = slice(h * HD, (h + 1) * HD)
            x = score[:, cols] * FACTOR + bias_ref[1]
            peak = jnp.maximum(stat_ref[j, 0:1, cols], down(jnp.max, x))
            own = jnp.exp2(stat_ref[j, 0:1, cols] - peak)
            e = jnp.exp2(x - peak)
            e_ref[j, :, cols] = e
            d_ref[j, :, cols] = d_prob[:, cols]
            out_ref[j, 0:1, cols] = peak
            out_ref[j, 1:2, cols] = stat_ref[j, 1:2, cols] * own + down(jnp.sum, e)
            out_ref[j, 2:3, cols] = stat_ref[j, 2:3, cols] * own + down(jnp.sum, e * d_prob[:, cols])
            out_ref[j, 3:4, cols] = own


def score_kernel(odd_ref, q_ref, do_ref, stat_ref, even_far_ref, odd_far_ref, bias_ref,
                 prob_ref, ds_ref, terms_ref, far_ref, out_ref):
    odd = odd_ref[0] == 1
    far_ref[...] = jnp.where(odd, odd_far_ref[...], even_far_ref[...])
    def products(j):
        lanes = slice(j * HD, (j + 1) * HD)
        return dot(far_ref[0, :, lanes], heads(q_ref, j), NT), dot(far_ref[1, :, lanes], heads(do_ref, j), NT)

    def softmax(j, score, d_prob):
        for h in range(GROUPS):
            cols = slice(h * HD, (h + 1) * HD)
            x = score[:, cols] * FACTOR + bias_ref[0]
            peak = jnp.maximum(stat_ref[j, 0:1, cols], down(jnp.max, x))
            old = jnp.exp2(stat_ref[j, 0:1, cols] - peak)
            e = jnp.exp2(x - peak)
            inv = 1.0 / (stat_ref[j, 1:2, cols] * old + down(jnp.sum, e))
            delta = (stat_ref[j, 2:3, cols] * old + down(jnp.sum, e * d_prob[:, cols])) * inv
            a = e * inv
            prob_ref[j, :, cols] = a.astype(jnp.bfloat16)
            ds_ref[j, :, cols] = (a * (d_prob[:, cols] - delta)).astype(jnp.bfloat16)
            out_ref[j, 0:1, cols] = stat_ref[j, 3:4, cols] * old * inv
            out_ref[j, 1:2, cols] = delta
            out_ref[j, 2:3, cols] = old * inv

    def terms(j):
        lanes = slice(j * HD, (j + 1) * HD)
        terms_ref[0, :, lanes] = (SCALE * dot(ds_ref[j], heads(q_ref, j), NN)).astype(jnp.bfloat16)
        terms_ref[1, :, lanes] = dot(prob_ref[j], heads(do_ref, j), NN).astype(jnp.bfloat16)

    for j in range(KVH):
        pair = products(j)
        if j > 0:
            terms(j - 1)
        softmax(j, *pair)
    terms(KVH - 1)


def near_kernel(odd_ref, q_ref, do_ref, e_ref, d_ref, stat_ref, passed_ref, prob_ref, ds_ref, out_ref):
    even = odd_ref[0] == 0

    def weights(j):
        for h in range(GROUPS):
            cols = slice(h * HD, (h + 1) * HD)
            b = e_ref[j, :, cols] * stat_ref[j, 2:3, cols]
            prob_ref[j, :, cols] = b.astype(jnp.bfloat16)
            ds_ref[j, :, cols] = (b * (d_ref[j, :, cols] - stat_ref[j, 1:2, cols])).astype(jnp.bfloat16)

    def terms(j):
        lanes = slice(j * HD, (j + 1) * HD)
        key_terms = SCALE * dot(ds_ref[j], heads(q_ref, j), NN)
        value_terms = dot(prob_ref[j], heads(do_ref, j), NN)
        key_terms += jnp.where(even, passed_ref[0, :, lanes].astype(jnp.float32), 0.0)
        value_terms += jnp.where(even, passed_ref[1, :, lanes].astype(jnp.float32), 0.0)
        out_ref[0, :, lanes] = key_terms.astype(jnp.bfloat16)
        out_ref[1, :, lanes] = value_terms.astype(jnp.bfloat16)

    weights(0)
    for j in range(KVH):
        if j + 1 < KVH:
            weights(j + 1)
        terms(j)


def finish_kernel(q_ref, do_ref, own_ref, near_ref, far_ref, prob_ref, ds_ref, near_prob_ref, near_ds_ref,
                  e_ref, d_ref, stat_ref, att_ref, dq_ref, terms_ref):
    p_own = e_ref[...] * stat_ref[0:1, :]
    ds_own = (p_own * (d_ref[...] - stat_ref[1:2, :])).astype(jnp.bfloat16)
    p_own = p_own.astype(jnp.bfloat16)
    terms_ref[0] = SCALE * dot(ds_own, heads(q_ref, 0), NN)
    terms_ref[1] = dot(p_own, heads(do_ref, 0), NN)
    k3t = jnp.concatenate([far_ref[0], near_ref[0], own_ref[0]], axis=0).T
    v3t = jnp.concatenate([far_ref[1], near_ref[1], own_ref[1]], axis=0).T
    p3 = jnp.concatenate([prob_ref[...], near_prob_ref[...], p_own], axis=0)
    ds3 = jnp.concatenate([ds_ref[...], near_ds_ref[...], ds_own], axis=0)
    att = dot(v3t, p3, NN)
    dq = dot(k3t, ds3, NN) * SCALE
    for h in range(GROUPS):
        cols = slice(h * HD, (h + 1) * HD)
        att_ref[:, cols] = att[:, cols].T.astype(jnp.bfloat16)
        dq_ref[:, cols] = dq[:, cols].T.astype(jnp.bfloat16)


PAIR = jax.ShapeDtypeStruct((2, ROWS, CUT), jnp.bfloat16)
FULL = jax.ShapeDtypeStruct((ROWS, QH * HD), jnp.bfloat16)
SCORE = jax.ShapeDtypeStruct((KVH, ROWS, WIDE), jnp.float32)
TILE = jax.ShapeDtypeStruct((KVH, ROWS, WIDE), jnp.bfloat16)
STAT = jax.ShapeDtypeStruct((KVH, 8, WIDE), jnp.float32)
HEAD = pl.BlockSpec((ROWS, WIDE), lambda j: (0, j))
BOTH = pl.BlockSpec((2, ROWS, HD), lambda j: (0, 0, j))
LINE = pl.BlockSpec((None, ROWS, WIDE), lambda j: (j, 0, 0))
FEW = pl.BlockSpec((None, 8, WIDE), lambda j: (j, 0, 0))


def pack(keys, values, lengths):
    return pl.pallas_call(
        pack_kernel,
        out_shape=(PAIR, jax.ShapeDtypeStruct((1, DOCS), jnp.int32)),
        in_specs=[HBM] * 3,
        out_specs=(VMEM, VMEM),
        scratch_shapes=[pltpu.SemaphoreType.DMA((2 * PARTS + 1,))],
        name="pack",
        compiler_params=ROOM,
    )(pinned(keys), pinned(values), pinned(lengths))


def stage(start, lengths, queries, d_out, own):
    return pl.pallas_call(
        stage_kernel,
        out_shape=(jax.ShapeDtypeStruct((2, ROWS, ROWS), jnp.float32), FULL, FULL, SCORE, SCORE, STAT),
        in_specs=[SMEM, VMEM, HBM, HBM, VMEM],
        out_specs=(VMEM,) * 6,
        scratch_shapes=[pltpu.SemaphoreType.DMA((4,))],
        name="stage",
        compiler_params=ROOM,
        cost_estimate=cost(3),
    )(start, lengths, pinned(queries), pinned(d_out), own)


def near_scores(q, do, near, bias, stat):
    return pl.pallas_call(
        near_score_kernel,
        out_shape=(SCORE, SCORE, STAT),
        in_specs=[VMEM] * 5,
        out_specs=(VMEM,) * 3,
        name="near_scores",
        compiler_params=ROOM,
        cost_estimate=cost(2),
    )(q, do, near, bias, stat)


def scores(odd, q, do, stat, even_far, odd_far, bias):
    return pl.pallas_call(
        score_kernel,
        out_shape=(TILE, TILE, PAIR, PAIR, STAT),
        in_specs=[SMEM] + [VMEM] * 6,
        out_specs=(VMEM,) * 5,
        name="scores",
        compiler_params=ROOM,
        cost_estimate=cost(4),
    )(odd, q, do, stat, even_far, odd_far, bias)


def near_terms(odd, q, do, e_near, d_near, stat, passed):
    return pl.pallas_call(
        near_kernel,
        out_shape=(TILE, TILE, PAIR),
        in_specs=[SMEM] + [VMEM] * 6,
        out_specs=(VMEM,) * 3,
        name="near_terms",
        compiler_params=ROOM,
        cost_estimate=cost(3),
    )(odd, q, do, e_near, d_near, stat, passed)


def finish(q, do, own, near, far, prob, ds, near_prob, near_ds, e_own, d_own, stat):
    return pl.pallas_call(
        finish_kernel,
        grid=(KVH,),
        out_shape=(FULL, FULL, jax.ShapeDtypeStruct((2, ROWS, CUT), jnp.float32)),
        in_specs=[HEAD, HEAD, BOTH, BOTH, BOTH, LINE, LINE, LINE, LINE, LINE, LINE, FEW],
        out_specs=(HEAD, HEAD, BOTH),
        name="finish",
        compiler_params=ROOM,
        cost_estimate=cost(8),
    )(q, do, own, near, far, prob, ds, near_prob, near_ds, e_own, d_own, stat)


def body(queries, keys, values, d_out, lengths):
    own, lens = pack(keys, values, lengths.reshape(1, DOCS))
    near = shifted(own, 1)
    even_far = shifted(own, 2, 2)
    index = lax.axis_index(AXES).astype(jnp.int32).reshape(1)
    start = index * ROWS
    odd = index % 2
    bias, q, do, e_own, d_own, stat = stage(start, lens, queries, d_out, own)
    near, bias = lax.optimization_barrier((near, bias))
    odd_far = shifted(near, 1, 2)
    e_near, d_near, stat = near_scores(q, do, near, bias, stat)
    prob, ds, far_terms, far, stat = scores(odd, q, do, stat, even_far, odd_far, bias)
    passed = shifted(far_terms, -1, 2)
    far_back = shifted(far_terms, -2, 2)
    near_prob, near_ds, near_out = near_terms(odd, q, do, e_near, d_near, stat, passed)
    near_back = shifted(near_out, -1)
    attended, d_queries, terms = finish(
        q, do, own, near, far, prob, ds, near_prob, near_ds, e_own, d_own, stat)
    d_keys = terms[0] + near_back[0].astype(jnp.float32) + far_back[0].astype(jnp.float32)
    d_values = terms[1] + near_back[1].astype(jnp.float32) + far_back[1].astype(jnp.float32)
    return attended, d_queries, d_keys.astype(jnp.bfloat16), d_values.astype(jnp.bfloat16)


def solution(mesh):
    split = P(AXES, None)
    return jax.shard_map(
        body,
        mesh=mesh,
        in_specs=(split, split, split, split, P()),
        out_specs=(split, split, split, split),
        check_vma=False,
    )
```

```python
import jax
import jax.numpy as jnp
from jax import lax
from jax.experimental import pallas as pl
from jax.experimental.pallas import tpu as pltpu
from jax.sharding import PartitionSpec as P

QH = 28
KVH = 4
GROUPS = QH // KVH
HD = 128
ROWS = 128
DOCS = 512
PARTS = 4
AXES = ("ctx", "dp")
NEG = -1e30
SCALE = HD**-0.5
FACTOR = SCALE * 1.4426950408889634
WIDE = GROUPS * HD
CUT = KVH * HD

NT = (((1,), (1,)), ((), ()))
NN = (((1,), (0,)), ((), ()))
VMEM = pl.BlockSpec(memory_space=pltpu.VMEM)
SMEM = pl.BlockSpec(memory_space=pltpu.SMEM)
HBM = pl.BlockSpec(memory_space=pltpu.HBM)
ROOM = pltpu.CompilerParams(vmem_limit_bytes=32 * 1024 * 1024)


def dot(a, b, dims):
    return lax.dot_general(a, b, dims, preferred_element_type=jnp.float32)


def shifted(value, steps, every=1):
    count = lax.axis_size(AXES)
    leading, last = (max(0, -steps), min(count, count - steps))
    return lax.ppermute(value, AXES, [(source, source + steps) for source in range(leading, last, every)])


def pinned(value):
    return pltpu.with_memory_space_constraint(value, pltpu.HBM)


def cost(us):
    return pl.CostEstimate(flops=0, bytes_accessed=int(us * 3_000_000), transcendentals=0)


def triangle(width):
    s = lax.broadcasted_iota(jnp.int32, (ROWS, width), 0)
    t = lax.broadcasted_iota(jnp.int32, (ROWS, width), 1) % HD
    return s <= t


def pack_kernel(k_ref, v_ref, lengths_ref, out_ref, len_ref, sems):
    copies = [pltpu.make_async_copy(lengths_ref, len_ref, sems.at[2 * PARTS])]
    for i, ref in enumerate((k_ref, v_ref)):
        for part in range(PARTS):
            rows = slice(part * ROWS // PARTS, (part + 1) * ROWS // PARTS)
            copies.append(pltpu.make_async_copy(ref.at[rows], out_ref.at[i, rows], sems.at[i * PARTS + part]))
    for copy in copies:
        copy.start()
    for copy in copies:
        copy.wait()


def heads(ref, j):
    first = j * GROUPS
    return jnp.concatenate([ref[:, h * HD:(h + 1) * HD] for h in range(first, first + GROUPS)], axis=0)


def down(fold, x):
    return fold(x, axis=0, keepdims=True)


def stage_kernel(start_ref, len_ref, q_in, do_in, kv_ref,
                 bias_ref, live_ref, q_ref, do_ref, e_ref, d_ref, stat_ref, sems):
    copies = []
    for i, wide in enumerate((slice(0, WIDE), slice(WIDE, KVH * WIDE))):
        copies.append(pltpu.make_async_copy(q_in.at[:, wide], q_ref.at[:, wide], sems.at[2 * i]))
        copies.append(pltpu.make_async_copy(do_in.at[:, wide], do_ref.at[:, wide], sems.at[2 * i + 1]))
    for copy in copies:
        copy.start()
    start = start_ref[0]
    lens = jnp.broadcast_to(len_ref[...].astype(jnp.float32), (ROWS, DOCS)).astype(jnp.bfloat16)
    doc = lax.broadcasted_iota(jnp.int32, (DOCS, DOCS), 0)
    upto = lax.broadcasted_iota(jnp.int32, (DOCS, DOCS), 1)
    before = jnp.where(upto <= doc, 1.0, 0.0).astype(jnp.bfloat16)
    ends = dot(before, lens, NT).astype(jnp.int32)
    query = start + lax.broadcasted_iota(jnp.int32, (DOCS, ROWS), 1)
    first = down(jnp.max, jnp.where(ends <= query, ends, 0)) - start
    s = lax.broadcasted_iota(jnp.int32, (ROWS, ROWS), 0)
    t = lax.broadcasted_iota(jnp.int32, (ROWS, ROWS), 1)
    own_bias = jnp.where((s <= t) & (s >= first), 0.0, NEG)
    far_bias = jnp.where((s > t) & (s - 2 * ROWS >= first), 0.0, NEG)
    bias_ref[0] = far_bias
    live_ref[...] = jnp.broadcast_to(jnp.max(down(jnp.max, far_bias), axis=1, keepdims=True), (8, HD))
    bias_ref[1] = jnp.where(s - ROWS >= first, 0.0, NEG)
    for j in range(KVH):
        lanes = slice(j * HD, (j + 1) * HD)
        if j < 2:
            copies[2 * j].wait()
            copies[2 * j + 1].wait()
        score = dot(kv_ref[0, :, lanes], heads(q_ref, j), NT)
        d_prob = dot(kv_ref[1, :, lanes], heads(do_ref, j), NT)
        for h in range(GROUPS):
            cols = slice(h * HD, (h + 1) * HD)
            x = score[:, cols] * FACTOR + own_bias
            peak = down(jnp.max, x)
            e = jnp.exp2(x - peak)
            e_ref[j, :, cols] = e
            d_ref[j, :, cols] = d_prob[:, cols]
            stat_ref[j, 0:1, cols] = peak
            stat_ref[j, 1:2, cols] = down(jnp.sum, e)
            stat_ref[j, 2:3, cols] = down(jnp.sum, e * d_prob[:, cols])


def near_score_kernel(q_ref, do_ref, near_ref, bias_ref, stat_ref, e_ref, d_ref, out_ref):
    for j in range(KVH):
        lanes = slice(j * HD, (j + 1) * HD)
        score = dot(near_ref[0, :, lanes], heads(q_ref, j), NT)
        d_prob = dot(near_ref[1, :, lanes], heads(do_ref, j), NT)
        for h in range(GROUPS):
            cols = slice(h * HD, (h + 1) * HD)
            x = score[:, cols] * FACTOR + bias_ref[1]
            peak = jnp.maximum(stat_ref[j, 0:1, cols], down(jnp.max, x))
            own = jnp.exp2(stat_ref[j, 0:1, cols] - peak)
            e = jnp.exp2(x - peak)
            e_ref[j, :, cols] = e
            d_ref[j, :, cols] = d_prob[:, cols]
            out_ref[j, 0:1, cols] = peak
            out_ref[j, 1:2, cols] = stat_ref[j, 1:2, cols] * own + down(jnp.sum, e)
            out_ref[j, 2:3, cols] = stat_ref[j, 2:3, cols] * own + down(jnp.sum, e * d_prob[:, cols])
            out_ref[j, 3:4, cols] = own


def score_kernel(odd_ref, live_ref, q_ref, do_ref, stat_ref, even_far_ref, odd_far_ref, bias_ref,
                 prob_ref, ds_ref, terms_ref, far_ref, out_ref):
    odd = odd_ref[0] == 1
    far_ref[...] = jnp.where(odd, odd_far_ref[...], even_far_ref[...])
    def products(j):
        lanes = slice(j * HD, (j + 1) * HD)
        return dot(far_ref[0, :, lanes], heads(q_ref, j), NT), dot(far_ref[1, :, lanes], heads(do_ref, j), NT)

    def softmax(j, score, d_prob):
        for h in range(GROUPS):
            cols = slice(h * HD, (h + 1) * HD)
            x = score[:, cols] * FACTOR + bias_ref[0]
            peak = jnp.maximum(stat_ref[j, 0:1, cols], down(jnp.max, x))
            old = jnp.exp2(stat_ref[j, 0:1, cols] - peak)
            e = jnp.exp2(x - peak)
            inv = 1.0 / (stat_ref[j, 1:2, cols] * old + down(jnp.sum, e))
            delta = (stat_ref[j, 2:3, cols] * old + down(jnp.sum, e * d_prob[:, cols])) * inv
            a = e * inv
            prob_ref[j, :, cols] = a.astype(jnp.bfloat16)
            ds_ref[j, :, cols] = (a * (d_prob[:, cols] - delta)).astype(jnp.bfloat16)
            out_ref[j, 0:1, cols] = stat_ref[j, 3:4, cols] * old * inv
            out_ref[j, 1:2, cols] = delta
            out_ref[j, 2:3, cols] = old * inv

    def terms(j):
        lanes = slice(j * HD, (j + 1) * HD)
        terms_ref[0, :, lanes] = (SCALE * dot(ds_ref[j], heads(q_ref, j), NN)).astype(jnp.bfloat16)
        terms_ref[1, :, lanes] = dot(prob_ref[j], heads(do_ref, j), NN).astype(jnp.bfloat16)

    live = jnp.max(live_ref[...]) > 0.5 * NEG

    @pl.when(live)
    def _():
        for j in range(KVH):
            pair = products(j)
            if j > 0:
                terms(j - 1)
            softmax(j, *pair)
        terms(KVH - 1)

    @pl.when(jnp.logical_not(live))
    def _():
        prob_ref[...] = jnp.zeros_like(prob_ref)
        ds_ref[...] = jnp.zeros_like(ds_ref)
        terms_ref[...] = jnp.zeros_like(terms_ref)
        for j in range(KVH):
            inv = 1.0 / stat_ref[j, 1:2, :]
            out_ref[j, 0:1, :] = stat_ref[j, 3:4, :] * inv
            out_ref[j, 1:2, :] = stat_ref[j, 2:3, :] * inv
            out_ref[j, 2:3, :] = inv


def near_kernel(q_ref, do_ref, e_ref, d_ref, stat_ref, prob_ref, ds_ref, out_ref):
    def weights(j):
        for h in range(GROUPS):
            cols = slice(h * HD, (h + 1) * HD)
            b = e_ref[j, :, cols] * stat_ref[j, 2:3, cols]
            prob_ref[j, :, cols] = b.astype(jnp.bfloat16)
            ds_ref[j, :, cols] = (b * (d_ref[j, :, cols] - stat_ref[j, 1:2, cols])).astype(jnp.bfloat16)

    def terms(j):
        lanes = slice(j * HD, (j + 1) * HD)
        out_ref[0, :, lanes] = SCALE * dot(ds_ref[j], heads(q_ref, j), NN)
        out_ref[1, :, lanes] = dot(prob_ref[j], heads(do_ref, j), NN)

    weights(0)
    for j in range(KVH):
        if j + 1 < KVH:
            weights(j + 1)
        terms(j)


def add_kernel(odd_ref, terms_ref, passed_ref, out_ref):
    passed = jnp.where(odd_ref[0] == 0, passed_ref[...].astype(jnp.float32), 0.0)
    out_ref[...] = (terms_ref[...] + passed).astype(jnp.bfloat16)


def finish_kernel(q_ref, do_ref, own_ref, near_ref, far_ref, prob_ref, ds_ref, near_prob_ref, near_ds_ref,
                  e_ref, d_ref, stat_ref, att_ref, dq_ref, terms_ref):
    p_own = e_ref[...] * stat_ref[0:1, :]
    ds_own = (p_own * (d_ref[...] - stat_ref[1:2, :])).astype(jnp.bfloat16)
    p_own = p_own.astype(jnp.bfloat16)
    terms_ref[0] = SCALE * dot(ds_own, heads(q_ref, 0), NN)
    terms_ref[1] = dot(p_own, heads(do_ref, 0), NN)
    k3t = jnp.concatenate([far_ref[0], near_ref[0], own_ref[0]], axis=0).T
    v3t = jnp.concatenate([far_ref[1], near_ref[1], own_ref[1]], axis=0).T
    p3 = jnp.concatenate([prob_ref[...], near_prob_ref[...], p_own], axis=0)
    ds3 = jnp.concatenate([ds_ref[...], near_ds_ref[...], ds_own], axis=0)
    att = dot(v3t, p3, NN)
    dq = dot(k3t, ds3, NN) * SCALE
    for h in range(GROUPS):
        cols = slice(h * HD, (h + 1) * HD)
        att_ref[:, cols] = att[:, cols].T.astype(jnp.bfloat16)
        dq_ref[:, cols] = dq[:, cols].T.astype(jnp.bfloat16)


PAIR = jax.ShapeDtypeStruct((2, ROWS, CUT), jnp.bfloat16)
FULL = jax.ShapeDtypeStruct((ROWS, QH * HD), jnp.bfloat16)
SCORE = jax.ShapeDtypeStruct((KVH, ROWS, WIDE), jnp.float32)
SUMS = jax.ShapeDtypeStruct((2, ROWS, CUT), jnp.float32)
TILE = jax.ShapeDtypeStruct((KVH, ROWS, WIDE), jnp.bfloat16)
FLAG = jax.ShapeDtypeStruct((8, HD), jnp.float32)
STAT = jax.ShapeDtypeStruct((KVH, 8, WIDE), jnp.float32)
HEAD = pl.BlockSpec((ROWS, WIDE), lambda j: (0, j))
BOTH = pl.BlockSpec((2, ROWS, HD), lambda j: (0, 0, j))
LINE = pl.BlockSpec((None, ROWS, WIDE), lambda j: (j, 0, 0))
FEW = pl.BlockSpec((None, 8, WIDE), lambda j: (j, 0, 0))


def pack(keys, values, lengths):
    return pl.pallas_call(
        pack_kernel,
        out_shape=(PAIR, jax.ShapeDtypeStruct((1, DOCS), jnp.int32)),
        in_specs=[HBM] * 3,
        out_specs=(VMEM, VMEM),
        scratch_shapes=[pltpu.SemaphoreType.DMA((2 * PARTS + 1,))],
        name="pack",
        compiler_params=ROOM,
    )(pinned(keys), pinned(values), pinned(lengths))


def stage(start, lengths, queries, d_out, own):
    return pl.pallas_call(
        stage_kernel,
        out_shape=(jax.ShapeDtypeStruct((2, ROWS, ROWS), jnp.float32), FLAG, FULL, FULL, SCORE, SCORE, STAT),
        in_specs=[SMEM, VMEM, HBM, HBM, VMEM],
        out_specs=(VMEM,) * 7,
        scratch_shapes=[pltpu.SemaphoreType.DMA((4,))],
        name="stage",
        compiler_params=ROOM,
        cost_estimate=cost(3),
    )(start, lengths, pinned(queries), pinned(d_out), own)


def near_scores(q, do, near, bias, stat):
    return pl.pallas_call(
        near_score_kernel,
        out_shape=(SCORE, SCORE, STAT),
        in_specs=[VMEM] * 5,
        out_specs=(VMEM,) * 3,
        name="near_scores",
        compiler_params=ROOM,
        cost_estimate=cost(2),
    )(q, do, near, bias, stat)


def scores(odd, live, q, do, stat, even_far, odd_far, bias):
    return pl.pallas_call(
        score_kernel,
        out_shape=(TILE, TILE, PAIR, PAIR, STAT),
        in_specs=[SMEM] + [VMEM] * 7,
        out_specs=(VMEM,) * 5,
        name="scores",
        compiler_params=ROOM,
        cost_estimate=cost(4),
    )(odd, live, q, do, stat, even_far, odd_far, bias)


def near_terms(q, do, e_near, d_near, stat):
    return pl.pallas_call(
        near_kernel,
        out_shape=(TILE, TILE, SUMS),
        in_specs=[VMEM] * 5,
        out_specs=(VMEM,) * 3,
        name="near_terms",
        compiler_params=ROOM,
        cost_estimate=cost(1),
    )(q, do, e_near, d_near, stat)


def add_passed(odd, terms, passed):
    return pl.pallas_call(
        add_kernel,
        out_shape=PAIR,
        in_specs=[SMEM, VMEM, VMEM],
        out_specs=VMEM,
        name="add_passed",
        compiler_params=ROOM,
        cost_estimate=cost(0.1),
    )(odd, terms, passed)


def finish(q, do, own, near, far, prob, ds, near_prob, near_ds, e_own, d_own, stat):
    return pl.pallas_call(
        finish_kernel,
        grid=(KVH,),
        out_shape=(FULL, FULL, SUMS),
        in_specs=[HEAD, HEAD, BOTH, BOTH, BOTH, LINE, LINE, LINE, LINE, LINE, LINE, FEW],
        out_specs=(HEAD, HEAD, BOTH),
        name="finish",
        compiler_params=ROOM,
        cost_estimate=cost(8),
    )(q, do, own, near, far, prob, ds, near_prob, near_ds, e_own, d_own, stat)


def body(queries, keys, values, d_out, lengths):
    own, lens = pack(keys, values, lengths.reshape(1, DOCS))
    near = shifted(own, 1)
    even_far = shifted(own, 2, 2)
    index = lax.axis_index(AXES).astype(jnp.int32).reshape(1)
    start = index * ROWS
    odd = index % 2
    bias, live, q, do, e_own, d_own, stat = stage(start, lens, queries, d_out, own)
    near, bias = lax.optimization_barrier((near, bias))
    odd_far = shifted(near, 1, 2)
    e_near, d_near, stat = near_scores(q, do, near, bias, stat)
    prob, ds, far_terms, far, stat = scores(odd, live, q, do, stat, even_far, odd_far, bias)
    passed = shifted(far_terms, -1, 2)
    far_back = shifted(far_terms, -2, 2)
    near_prob, near_ds, near_out = near_terms(q, do, e_near, d_near, stat)
    near_back = shifted(add_passed(odd, near_out, passed), -1)
    attended, d_queries, terms = finish(
        q, do, own, near, far, prob, ds, near_prob, near_ds, e_own, d_own, stat)
    d_keys = terms[0] + near_back[0].astype(jnp.float32) + far_back[0].astype(jnp.float32)
    d_values = terms[1] + near_back[1].astype(jnp.float32) + far_back[1].astype(jnp.float32)
    return attended, d_queries, d_keys.astype(jnp.bfloat16), d_values.astype(jnp.bfloat16)


def solution(mesh):
    split = P(AXES, None)
    return jax.shard_map(
        body,
        mesh=mesh,
        in_specs=(split, split, split, split, P()),
        out_specs=(split, split, split, split),
        check_vma=False,
    )
```

```python
import jax
import jax.numpy as jnp
from jax import lax
from jax.experimental import pallas as pl
from jax.experimental.pallas import tpu as pltpu
from jax.sharding import PartitionSpec as P

QH = 28
KVH = 4
GROUPS = QH // KVH
HD = 128
ROWS = 128
DOCS = 512
PARTS = 4
AXES = ("ctx", "dp")
NEG = -1e30
SCALE = HD**-0.5
FACTOR = SCALE * 1.4426950408889634
WIDE = GROUPS * HD
CUT = KVH * HD

NT = (((1,), (1,)), ((), ()))
NN = (((1,), (0,)), ((), ()))
VMEM = pl.BlockSpec(memory_space=pltpu.VMEM)
SMEM = pl.BlockSpec(memory_space=pltpu.SMEM)
HBM = pl.BlockSpec(memory_space=pltpu.HBM)
ROOM = pltpu.CompilerParams(vmem_limit_bytes=32 * 1024 * 1024)


def dot(a, b, dims):
    return lax.dot_general(a, b, dims, preferred_element_type=jnp.float32)


def shifted(value, steps, every=1):
    count = lax.axis_size(AXES)
    leading, last = (max(0, -steps), min(count, count - steps))
    return lax.ppermute(value, AXES, [(source, source + steps) for source in range(leading, last, every)])


def pinned(value):
    return pltpu.with_memory_space_constraint(value, pltpu.HBM)


def cost(us):
    return pl.CostEstimate(flops=0, bytes_accessed=int(us * 3_000_000), transcendentals=0)


def triangle(width):
    s = lax.broadcasted_iota(jnp.int32, (ROWS, width), 0)
    t = lax.broadcasted_iota(jnp.int32, (ROWS, width), 1) % HD
    return s <= t


def pack_kernel(k_ref, v_ref, lengths_ref, out_ref, len_ref, sems):
    copies = [pltpu.make_async_copy(lengths_ref, len_ref, sems.at[2 * PARTS])]
    for i, ref in enumerate((k_ref, v_ref)):
        for part in range(PARTS):
            rows = slice(part * ROWS // PARTS, (part + 1) * ROWS // PARTS)
            copies.append(pltpu.make_async_copy(ref.at[rows], out_ref.at[i, rows], sems.at[i * PARTS + part]))
    for copy in copies:
        copy.start()
    for copy in copies:
        copy.wait()


def heads(ref, j):
    first = j * GROUPS
    return jnp.concatenate([ref[:, h * HD:(h + 1) * HD] for h in range(first, first + GROUPS)], axis=0)


def down(fold, x):
    return fold(x, axis=0, keepdims=True)


def stage_kernel(start_ref, len_ref, q_in, do_in, kv_ref,
                 bias_ref, live_ref, q_ref, do_ref, e_ref, d_ref, stat_ref, sems):
    copies = []
    for i, wide in enumerate((slice(0, WIDE), slice(WIDE, KVH * WIDE))):
        copies.append(pltpu.make_async_copy(q_in.at[:, wide], q_ref.at[:, wide], sems.at[2 * i]))
        copies.append(pltpu.make_async_copy(do_in.at[:, wide], do_ref.at[:, wide], sems.at[2 * i + 1]))
    for copy in copies:
        copy.start()
    start = start_ref[0]
    lens = jnp.broadcast_to(len_ref[...].astype(jnp.float32), (ROWS, DOCS)).astype(jnp.bfloat16)
    doc = lax.broadcasted_iota(jnp.int32, (DOCS, DOCS), 0)
    upto = lax.broadcasted_iota(jnp.int32, (DOCS, DOCS), 1)
    before = jnp.where(upto <= doc, 1.0, 0.0).astype(jnp.bfloat16)
    ends = dot(before, lens, NT).astype(jnp.int32)
    query = start + lax.broadcasted_iota(jnp.int32, (DOCS, ROWS), 1)
    first = down(jnp.max, jnp.where(ends <= query, ends, 0)) - start
    s = lax.broadcasted_iota(jnp.int32, (ROWS, ROWS), 0)
    t = lax.broadcasted_iota(jnp.int32, (ROWS, ROWS), 1)
    own_bias = jnp.where((s <= t) & (s >= first), 0.0, NEG)
    far_bias = jnp.where((s > t) & (s - 2 * ROWS >= first), 0.0, NEG)
    bias_ref[0] = far_bias
    live_ref[...] = jnp.broadcast_to(jnp.max(down(jnp.max, far_bias), axis=1, keepdims=True), (8, HD))
    bias_ref[1] = jnp.where(s - ROWS >= first, 0.0, NEG)
    for j in range(KVH):
        lanes = slice(j * HD, (j + 1) * HD)
        if j < 2:
            copies[2 * j].wait()
            copies[2 * j + 1].wait()
        score = dot(kv_ref[0, :, lanes], heads(q_ref, j), NT)
        d_prob = dot(kv_ref[1, :, lanes], heads(do_ref, j), NT)
        for h in range(GROUPS):
            cols = slice(h * HD, (h + 1) * HD)
            x = score[:, cols] * FACTOR + own_bias
            peak = down(jnp.max, x)
            e = jnp.exp2(x - peak)
            e_ref[j, :, cols] = e
            d_ref[j, :, cols] = d_prob[:, cols]
            stat_ref[j, 0:1, cols] = peak
            stat_ref[j, 1:2, cols] = down(jnp.sum, e)
            stat_ref[j, 2:3, cols] = down(jnp.sum, e * d_prob[:, cols])


def near_score_kernel(q_ref, do_ref, near_ref, bias_ref, stat_ref, e_ref, d_ref, out_ref):
    for j in range(KVH):
        lanes = slice(j * HD, (j + 1) * HD)
        score = dot(near_ref[0, :, lanes], heads(q_ref, j), NT)
        d_prob = dot(near_ref[1, :, lanes], heads(do_ref, j), NT)
        for h in range(GROUPS):
            cols = slice(h * HD, (h + 1) * HD)
            x = score[:, cols] * FACTOR + bias_ref[1]
            peak = jnp.maximum(stat_ref[j, 0:1, cols], down(jnp.max, x))
            own = jnp.exp2(stat_ref[j, 0:1, cols] - peak)
            e = jnp.exp2(x - peak)
            e_ref[j, :, cols] = e
            d_ref[j, :, cols] = d_prob[:, cols]
            out_ref[j, 0:1, cols] = peak
            out_ref[j, 1:2, cols] = stat_ref[j, 1:2, cols] * own + down(jnp.sum, e)
            out_ref[j, 2:3, cols] = stat_ref[j, 2:3, cols] * own + down(jnp.sum, e * d_prob[:, cols])
            out_ref[j, 3:4, cols] = own


def score_kernel(odd_ref, live_ref, q_ref, do_ref, stat_ref, even_far_ref, odd_far_ref, bias_ref,
                 prob_ref, ds_ref, terms_ref, far_ref, out_ref):
    odd = odd_ref[0] == 1
    far_ref[...] = jnp.where(odd, odd_far_ref[...], even_far_ref[...])
    def products(j):
        lanes = slice(j * HD, (j + 1) * HD)
        return dot(far_ref[0, :, lanes], heads(q_ref, j), NT), dot(far_ref[1, :, lanes], heads(do_ref, j), NT)

    def softmax(j, score, d_prob):
        for h in range(GROUPS):
            cols = slice(h * HD, (h + 1) * HD)
            x = score[:, cols] * FACTOR + bias_ref[0]
            peak = jnp.maximum(stat_ref[j, 0:1, cols], down(jnp.max, x))
            old = jnp.exp2(stat_ref[j, 0:1, cols] - peak)
            e = jnp.exp2(x - peak)
            inv = 1.0 / (stat_ref[j, 1:2, cols] * old + down(jnp.sum, e))
            delta = (stat_ref[j, 2:3, cols] * old + down(jnp.sum, e * d_prob[:, cols])) * inv
            a = e * inv
            prob_ref[j, :, cols] = a.astype(jnp.bfloat16)
            ds_ref[j, :, cols] = (a * (d_prob[:, cols] - delta)).astype(jnp.bfloat16)
            out_ref[j, 0:1, cols] = stat_ref[j, 3:4, cols] * old * inv
            out_ref[j, 1:2, cols] = delta
            out_ref[j, 2:3, cols] = old * inv

    def terms(j):
        lanes = slice(j * HD, (j + 1) * HD)
        both = dot(jnp.concatenate([ds_ref[j], prob_ref[j]], axis=0),
                   jnp.concatenate([heads(q_ref, j), heads(do_ref, j)], axis=1), NN)
        terms_ref[0, :, lanes] = (SCALE * both[:ROWS, :HD]).astype(jnp.bfloat16)
        terms_ref[1, :, lanes] = both[ROWS:, HD:].astype(jnp.bfloat16)

    live = jnp.max(live_ref[...]) > 0.5 * NEG

    @pl.when(live)
    def _():
        for j in range(KVH):
            pair = products(j)
            if j > 0:
                terms(j - 1)
            softmax(j, *pair)
        terms(KVH - 1)

    @pl.when(jnp.logical_not(live))
    def _():
        prob_ref[...] = jnp.zeros_like(prob_ref)
        ds_ref[...] = jnp.zeros_like(ds_ref)
        terms_ref[...] = jnp.zeros_like(terms_ref)
        for j in range(KVH):
            inv = 1.0 / stat_ref[j, 1:2, :]
            out_ref[j, 0:1, :] = stat_ref[j, 3:4, :] * inv
            out_ref[j, 1:2, :] = stat_ref[j, 2:3, :] * inv
            out_ref[j, 2:3, :] = inv


def near_kernel(q_ref, do_ref, e_ref, d_ref, stat_ref, prob_ref, ds_ref, out_ref):
    def weights(j):
        for h in range(GROUPS):
            cols = slice(h * HD, (h + 1) * HD)
            b = e_ref[j, :, cols] * stat_ref[j, 2:3, cols]
            prob_ref[j, :, cols] = b.astype(jnp.bfloat16)
            ds_ref[j, :, cols] = (b * (d_ref[j, :, cols] - stat_ref[j, 1:2, cols])).astype(jnp.bfloat16)

    def terms(j):
        lanes = slice(j * HD, (j + 1) * HD)
        out_ref[0, :, lanes] = SCALE * dot(ds_ref[j], heads(q_ref, j), NN)
        out_ref[1, :, lanes] = dot(prob_ref[j], heads(do_ref, j), NN)

    weights(0)
    for j in range(KVH):
        if j + 1 < KVH:
            weights(j + 1)
        terms(j)


def add_kernel(odd_ref, terms_ref, passed_ref, out_ref):
    passed = jnp.where(odd_ref[0] == 0, passed_ref[...].astype(jnp.float32), 0.0)
    out_ref[...] = (terms_ref[...] + passed).astype(jnp.bfloat16)


def finish_kernel(q_ref, do_ref, own_ref, near_ref, far_ref, prob_ref, ds_ref, near_prob_ref, near_ds_ref,
                  e_ref, d_ref, stat_ref, att_ref, dq_ref, terms_ref):
    p_own = e_ref[...] * stat_ref[0:1, :]
    ds_own = (p_own * (d_ref[...] - stat_ref[1:2, :])).astype(jnp.bfloat16)
    p_own = p_own.astype(jnp.bfloat16)
    terms_ref[0] = SCALE * dot(ds_own, heads(q_ref, 0), NN)
    terms_ref[1] = dot(p_own, heads(do_ref, 0), NN)
    k3t = jnp.concatenate([far_ref[0], near_ref[0], own_ref[0]], axis=0).T
    v3t = jnp.concatenate([far_ref[1], near_ref[1], own_ref[1]], axis=0).T
    p3 = jnp.concatenate([prob_ref[...], near_prob_ref[...], p_own], axis=0)
    ds3 = jnp.concatenate([ds_ref[...], near_ds_ref[...], ds_own], axis=0)
    att = dot(v3t, p3, NN)
    dq = dot(k3t, ds3, NN) * SCALE
    for h in range(GROUPS):
        cols = slice(h * HD, (h + 1) * HD)
        att_ref[:, cols] = att[:, cols].T.astype(jnp.bfloat16)
        dq_ref[:, cols] = dq[:, cols].T.astype(jnp.bfloat16)


PAIR = jax.ShapeDtypeStruct((2, ROWS, CUT), jnp.bfloat16)
FULL = jax.ShapeDtypeStruct((ROWS, QH * HD), jnp.bfloat16)
SCORE = jax.ShapeDtypeStruct((KVH, ROWS, WIDE), jnp.float32)
SUMS = jax.ShapeDtypeStruct((2, ROWS, CUT), jnp.float32)
TILE = jax.ShapeDtypeStruct((KVH, ROWS, WIDE), jnp.bfloat16)
FLAG = jax.ShapeDtypeStruct((8, HD), jnp.float32)
STAT = jax.ShapeDtypeStruct((KVH, 8, WIDE), jnp.float32)
HEAD = pl.BlockSpec((ROWS, WIDE), lambda j: (0, j))
BOTH = pl.BlockSpec((2, ROWS, HD), lambda j: (0, 0, j))
LINE = pl.BlockSpec((None, ROWS, WIDE), lambda j: (j, 0, 0))
FEW = pl.BlockSpec((None, 8, WIDE), lambda j: (j, 0, 0))


def pack(keys, values, lengths):
    return pl.pallas_call(
        pack_kernel,
        out_shape=(PAIR, jax.ShapeDtypeStruct((1, DOCS), jnp.int32)),
        in_specs=[HBM] * 3,
        out_specs=(VMEM, VMEM),
        scratch_shapes=[pltpu.SemaphoreType.DMA((2 * PARTS + 1,))],
        name="pack",
        compiler_params=ROOM,
    )(pinned(keys), pinned(values), pinned(lengths))


def stage(start, lengths, queries, d_out, own):
    return pl.pallas_call(
        stage_kernel,
        out_shape=(jax.ShapeDtypeStruct((2, ROWS, ROWS), jnp.float32), FLAG, FULL, FULL, SCORE, SCORE, STAT),
        in_specs=[SMEM, VMEM, HBM, HBM, VMEM],
        out_specs=(VMEM,) * 7,
        scratch_shapes=[pltpu.SemaphoreType.DMA((4,))],
        name="stage",
        compiler_params=ROOM,
        cost_estimate=cost(3),
    )(start, lengths, pinned(queries), pinned(d_out), own)


def near_scores(q, do, near, bias, stat):
    return pl.pallas_call(
        near_score_kernel,
        out_shape=(SCORE, SCORE, STAT),
        in_specs=[VMEM] * 5,
        out_specs=(VMEM,) * 3,
        name="near_scores",
        compiler_params=ROOM,
        cost_estimate=cost(2),
    )(q, do, near, bias, stat)


def scores(odd, live, q, do, stat, even_far, odd_far, bias):
    return pl.pallas_call(
        score_kernel,
        out_shape=(TILE, TILE, PAIR, PAIR, STAT),
        in_specs=[SMEM] + [VMEM] * 7,
        out_specs=(VMEM,) * 5,
        name="scores",
        compiler_params=ROOM,
        cost_estimate=cost(4),
    )(odd, live, q, do, stat, even_far, odd_far, bias)


def near_terms(q, do, e_near, d_near, stat):
    return pl.pallas_call(
        near_kernel,
        out_shape=(TILE, TILE, SUMS),
        in_specs=[VMEM] * 5,
        out_specs=(VMEM,) * 3,
        name="near_terms",
        compiler_params=ROOM,
        cost_estimate=cost(1),
    )(q, do, e_near, d_near, stat)


def add_passed(odd, terms, passed):
    return pl.pallas_call(
        add_kernel,
        out_shape=PAIR,
        in_specs=[SMEM, VMEM, VMEM],
        out_specs=VMEM,
        name="add_passed",
        compiler_params=ROOM,
        cost_estimate=cost(0.1),
    )(odd, terms, passed)


def finish(q, do, own, near, far, prob, ds, near_prob, near_ds, e_own, d_own, stat):
    return pl.pallas_call(
        finish_kernel,
        grid=(KVH,),
        out_shape=(FULL, FULL, SUMS),
        in_specs=[HEAD, HEAD, BOTH, BOTH, BOTH, LINE, LINE, LINE, LINE, LINE, LINE, FEW],
        out_specs=(HEAD, HEAD, BOTH),
        name="finish",
        compiler_params=ROOM,
        cost_estimate=cost(8),
    )(q, do, own, near, far, prob, ds, near_prob, near_ds, e_own, d_own, stat)


def body(queries, keys, values, d_out, lengths):
    own, lens = pack(keys, values, lengths.reshape(1, DOCS))
    near = shifted(own, 1)
    even_far = shifted(own, 2, 2)
    index = lax.axis_index(AXES).astype(jnp.int32).reshape(1)
    start = index * ROWS
    odd = index % 2
    bias, live, q, do, e_own, d_own, stat = stage(start, lens, queries, d_out, own)
    near, bias = lax.optimization_barrier((near, bias))
    odd_far = shifted(near, 1, 2)
    e_near, d_near, stat = near_scores(q, do, near, bias, stat)
    prob, ds, far_terms, far, stat = scores(odd, live, q, do, stat, even_far, odd_far, bias)
    passed = shifted(far_terms, -1, 2)
    far_back = shifted(far_terms, -2, 2)
    near_prob, near_ds, near_out = near_terms(q, do, e_near, d_near, stat)
    near_back = shifted(add_passed(odd, near_out, passed), -1)
    attended, d_queries, terms = finish(
        q, do, own, near, far, prob, ds, near_prob, near_ds, e_own, d_own, stat)
    d_keys = terms[0] + near_back[0].astype(jnp.float32) + far_back[0].astype(jnp.float32)
    d_values = terms[1] + near_back[1].astype(jnp.float32) + far_back[1].astype(jnp.float32)
    return attended, d_queries, d_keys.astype(jnp.bfloat16), d_values.astype(jnp.bfloat16)


def solution(mesh):
    split = P(AXES, None)
    return jax.shard_map(
        body,
        mesh=mesh,
        in_specs=(split, split, split, split, P()),
        out_specs=(split, split, split, split),
        check_vma=False,
    )
```
